32 devices in a mesh: row: 8 (over y, x, core), col: 4 (over z).
Axes of the slice: x: 2, y: 2, z: 4, core: 2. Of those that a mesh axis runs over, the one named last changes fastest.
Arguments:
- ortho_in: bfloat16 [7168, 9216], P(('row', 'col')), may hold values from -6 to 6
Outputs:
- next_iterate: bfloat16 [7168, 9216], P(('row', 'col'))
The draws below stay inside these ranges and needn't reach their ends.
All inputs are finite; a program needn't handle non-finite values.
Results may differ from the reference program's by a relative error of at most 0.024.
Values may be sent and summed in bfloat16 or wider, within the bound.
No kernel may reach another device: no remote copies, remote signals or barrier semaphores. Data moves between devices by JAX's collectives and lax.ppermute only.
A program may use at most 128 MiB of HBM per device.

```python
import math
import jax
import jax.numpy as jnp
from jax import lax

D = 7168
FF = 9216
TC = 2304


def draw_ortho_in(key, part):
    key = jax.random.fold_in(key, 11)
    noise_key = jax.random.fold_in(key, 0)
    noise = jax.random.normal(noise_key, (D, FF), jnp.float32)
    values = jnp.clip(noise, -6.0, 6.0)
    return values.astype(jnp.bfloat16)


def setup_inputs(seed: int = 0) -> dict:
    key_of = jax.random.split(jax.random.key(seed), 2)
    ortho_in = draw_ortho_in(jax.random.fold_in(key_of[1], 71), 0)
    return dict(ortho_in=ortho_in)


coef_a = 3.4445
coef_b = -4.775
coef_c = 2.0315

def reference(ortho_in):
    ortho_f = ortho_in.astype(jnp.float32)
    inv_square = 1.0 / (math.sqrt(D) + math.sqrt(FF)) ** 2

    def add_block(index, total):
        block = lax.dynamic_slice_in_dim(ortho_f, (index * TC).astype(jnp.int32), TC, 1)
        partial_gram = jnp.dot(block, block.T, precision=lax.Precision.HIGHEST)
        rounded = lax.optimization_barrier(partial_gram.astype(jnp.bfloat16))
        return total + rounded.astype(jnp.float32)
    gram_sum = lax.fori_loop(0, FF // TC, add_block, jnp.zeros((D, D), jnp.float32))
    gram_f = (gram_sum * inv_square).astype(jnp.bfloat16).astype(jnp.float32)
    first_prod = jnp.dot(gram_f, ortho_f, precision=lax.Precision.HIGHEST).astype(jnp.bfloat16)
    second_prod = jnp.dot(gram_f, first_prod.astype(jnp.float32), precision=lax.Precision.HIGHEST)
    iterate = coef_a * ortho_f + coef_b * first_prod.astype(jnp.float32) + coef_c * second_prod
    return iterate.astype(jnp.bfloat16)
```

```python
import functools
import math

import jax
import jax.numpy as jnp
from jax import lax
from jax.experimental import pallas as pl
from jax.experimental.pallas import tpu as pltpu
from jax.sharding import PartitionSpec as P

coef_a = 3.4445
coef_b = -4.775
coef_c = 2.0315
bf16 = jnp.bfloat16
f32 = jnp.float32
VMEM_BYTES = 48 * 1024 * 1024


def widths_of(width, count):
    unit = 256 if width % 256 == 0 else 128
    base, extra = divmod(width // unit, count)
    return [unit * (base + (i >= count - extra)) for i in range(count)]


def dot_t(a, b):
    return lax.dot_general(a, b, (((1,), (1,)), ((), ())), preferred_element_type=f32)


def after(value, *others):
    return lax.optimization_barrier((value, *others))[0]


def swap(value, bit):
    count = lax.axis_size("row")
    return lax.ppermute(value, "row", [(r, r ^ bit) for r in range(count)])


def gather_chips(own):
    count = lax.axis_size("row")
    bit_x, bit_y = count // 4, count // 2
    h = own.shape[0] // 2
    corner = bit_x | bit_y
    parts = {(0, 0): own}
    parts[(bit_x, 0)] = swap(own, bit_x)
    parts[(bit_y, 0)] = swap(own, bit_y)
    from_x, from_y = lax.optimization_barrier((parts[(bit_x, 0)], parts[(bit_y, 0)]))
    upper, lower = lax.optimization_barrier((from_x[:h], from_y[h:]))
    parts[(corner, 0)] = swap(upper, bit_y)
    parts[(corner, h)] = swap(lower, bit_x)
    return parts, (upper, lower)


def add_cores(parts, hold=None):
    bit_x = lax.axis_size("row") // 4
    parts = dict(parts)
    bit = 1
    while bit < bit_x:
        for j, offset in list(parts):
            if (j | bit, offset) not in parts:
                part = parts[(j, offset)]
                if hold is not None:
                    part = after(part, hold)
                parts[(j | bit, offset)] = swap(part, bit)
        bit *= 2
    return parts


def whole_block(parts, j):
    pieces = [parts[key] for key in sorted(parts) if key[0] == j]
    return pieces[0] if len(pieces) == 1 else jnp.concatenate(pieces, axis=0)


def pair_kernel(count, low_ref, *refs):
    own, peer, out = refs[:count], refs[count : 2 * count], refs[2 * count]
    h = out.shape[0]

    def product(left, right, first):
        total = None
        for a, b in zip(left, right):
            term = dot_t(a[first : first + h, :], b[...])
            total = term if total is None else total + term
        out[...] = total.astype(bf16)

    @pl.when(low_ref[0] == 1)
    def _():
        product(own, peer, 0)

    @pl.when(low_ref[0] == 0)
    def _():
        product(peer, own, h)


def pair_piece(low, own, peer):
    size = own[0].shape[0]
    flops = size * size * sum(o.shape[1] for o in own)
    return pl.pallas_call(
        functools.partial(pair_kernel, len(own)),
        out_shape=jax.ShapeDtypeStruct((size // 2, size), bf16),
        in_specs=[pl.BlockSpec(memory_space=pltpu.SMEM)]
        + [pl.BlockSpec(memory_space=pltpu.VMEM)] * (2 * len(own)),
        out_specs=pl.BlockSpec(memory_space=pltpu.VMEM),
        cost_estimate=pl.CostEstimate(
            flops=flops, bytes_accessed=4 * flops // size, transcendentals=0
        ),
        compiler_params=pltpu.CompilerParams(vmem_limit_bytes=VMEM_BYTES),
    )(low, *own, *peer)


def block_kernel(low_ref, mine, theirs, gram_in, out):
    h = mine.shape[0]

    @pl.when(low_ref[0] == 1)
    def _():
        out[:h, :] = mine[...]
        out[h:, :] = theirs[...]

    @pl.when(low_ref[0] == 0)
    def _():
        out[...] = jnp.concatenate([theirs[...], mine[...]], axis=0).T


def put_block(gram, low, mine, theirs, j):
    h, size = mine.shape
    return pl.pallas_call(
        block_kernel,
        grid=(1,),
        out_shape=jax.ShapeDtypeStruct(gram.shape, bf16),
        in_specs=[
            pl.BlockSpec(memory_space=pltpu.SMEM),
            pl.BlockSpec((h, size), lambda i: (0, 0)),
            pl.BlockSpec((h, size), lambda i: (0, 0)),
            pl.BlockSpec(memory_space=pl.ANY),
        ],
        out_specs=pl.BlockSpec((None, size, size), lambda i: (j, 0, 0)),
        input_output_aliases={3: 0},
        cost_estimate=pl.CostEstimate(
            flops=0, bytes_accessed=4 * size * size, transcendentals=0
        ),
        compiler_params=pltpu.CompilerParams(vmem_limit_bytes=VMEM_BYTES),
    )(low, mine, theirs, gram)


def product_kernel(keys, start, finish, *refs):
    gram, parts = refs[0], refs[1 : 1 + len(keys)]
    extra = refs[1 + len(keys) : -5]
    out, gbuf, xbuf, acc, sems = refs[-5:]
    count, size, width = xbuf.shape
    h = size // 2

    def piece(j, part):
        return xbuf.at[j, pl.ds(part * h, h)], sems.at[j, part]

    copies = []
    for j in range(count):
        copies.append(pltpu.make_async_copy(gram.at[j], gbuf.at[j], sems.at[j, 2]))
        for part in range(2):
            key = (j, part * h) if (j, part * h) in keys else (j, 0)
            first = part * h - key[1]
            source = parts[keys.index(key)].at[pl.ds(first, h), pl.ds(start, width)]
            copies.append(pltpu.make_async_copy(source, *piece(j, part)))
    for copy in copies:
        copy.start()
    acc[...] = jnp.zeros_like(acc)

    @pl.loop(0, count)
    def _(j):
        pltpu.make_async_copy(gbuf.at[j], gbuf.at[j], sems.at[j, 2]).wait()
        for part in range(2):
            there, sem = piece(j, part)
            pltpu.make_async_copy(there, there, sem).wait()
        acc[...] += jnp.dot(gbuf[j], xbuf[j], preferred_element_type=f32)

    if finish:
        tile, first = extra
        out[...] = (
            coef_a * tile[...].astype(f32)
            + coef_b * first[...].astype(f32)
            + coef_c * acc[...]
        ).astype(bf16)
    else:
        out[...] = acc[...].astype(bf16)


def product(gram, parts, start, width, extra=()):
    count, size, _ = gram.shape
    keys = sorted(parts)
    flops = 2 * count * size * size * width
    return pl.pallas_call(
        functools.partial(product_kernel, keys, start, bool(extra)),
        out_shape=jax.ShapeDtypeStruct((size, width), bf16),
        in_specs=[pl.BlockSpec(memory_space=pl.ANY)] * (1 + len(keys))
        + [pl.BlockSpec(memory_space=pltpu.VMEM)] * len(extra),
        out_specs=pl.BlockSpec(memory_space=pltpu.VMEM),
        scratch_shapes=[
            pltpu.VMEM((count, size, size), bf16),
            pltpu.VMEM((count, size, width), bf16),
            pltpu.VMEM((size, width), f32),
            pltpu.SemaphoreType.DMA((count, 3)),
        ],
        cost_estimate=pl.CostEstimate(
            flops=flops,
            bytes_accessed=2 * count * size * (size + width),
            transcendentals=0,
        ),
        compiler_params=pltpu.CompilerParams(vmem_limit_bytes=VMEM_BYTES),
    )(gram, *[parts[key] for key in keys], *extra)


def sum_on_line(piece, scale, arrivals, depth):
    count = lax.axis_size("col")
    me = lax.axis_index("col")
    half = count // 2

    def send(stage, value, pairs):
        done = arrivals.setdefault(stage, [])
        if len(done) >= depth:
            value = after(value, done[-depth])
        arrived = lax.ppermute(value, "col", pairs)
        done.append(arrived)
        return arrived

    for s in range(half - 1):
        pairs = [(s, s + 1), (count - 1 - s, count - 2 - s)]
        arrived = send(s, piece, pairs)
        piece = (piece.astype(f32) + arrived.astype(f32)).astype(bf16)
    arrived = send(half - 1, piece, [(half - 1, half), (half, half - 1)])
    total = ((piece.astype(f32) + arrived.astype(f32)) * scale).astype(bf16)
    for s in range(half - 2, -1, -1):
        pairs = [(s + 1, s), (count - 2 - s, count - 1 - s)]
        arrived = send(2 * half - 2 - s, total, pairs)
        total = jnp.where((me == s) | (me == count - 1 - s), arrived, total)
    return total


def per_device(ortho_in):
    rows, cols = ortho_in.shape
    n_row = lax.axis_size("row")
    n_col = lax.axis_size("col")
    me = lax.axis_index("row")
    block = rows * n_col
    width = cols // n_col
    scale = 1.0 / (math.sqrt(block * n_row) + math.sqrt(cols)) ** 2
    h = block // 2
    bit_x, bit_y = n_row // 4, n_row // 2
    cores = range(1, bit_x)
    chips = (bit_x, bit_y, bit_x | bit_y)

    def exchange(value):
        return lax.all_to_all(value, "col", split_axis=0, concat_axis=0, tiled=True)

    tiles, gathered, siblings = [], [], []
    start = 0
    thirds = widths_of(width, 3)
    for w in (thirds[0], thirds[1] + thirds[2]):
        first = [start + c * width for c in range(n_col)]
        tile = exchange(jnp.concatenate([ortho_in[:, f : f + w] for f in first], axis=0))
        tiles.append(tile)
        parts, tied = gather_chips(tile)
        gathered.append(parts)
        siblings.append(add_cores({(0, 0): tile}))
        start += w

    arrivals = {}

    def low_of(j):
        return ((me & (1 << (j.bit_length() - 1))) == 0).astype(jnp.int32).reshape(1)

    own_sums = []
    for part in range(2):
        total = sum(dot_t(t[part * h : (part + 1) * h], t) for t in tiles)
        own_sums.append(sum_on_line(total.astype(bf16), scale, arrivals, 1))
    pieces = {}
    for j in cores:
        piece = pair_piece(low_of(j), tiles, [s[(j, 0)] for s in siblings])
        pieces[j, 0] = sum_on_line(piece, scale, arrivals, 1)
    for j in chips:
        peers = [whole_block(parts, j) for parts in gathered]
        if j != chips[-1]:
            peers[0] = after(peers[0], *tied)
        for i in range(bit_x):
            left = [s[(i, 0)] for s in siblings]
            piece = pair_piece(low_of(j), left, peers)
            pieces[j, i] = sum_on_line(piece, scale, arrivals, 2)
    gram = jnp.zeros((n_row, block, block), bf16)
    for (j, i), mine in pieces.items():
        if j not in chips:
            gram = put_block(gram, low_of(j), mine, swap(mine, j), j)
            continue
        theirs = swap(mine, j)
        if i > 0:
            mine = swap(mine, i)
        gram = put_block(gram, low_of(j), mine, theirs, j | i)
    for part in range(2):
        gram = lax.dynamic_update_slice(gram, own_sums[part][None], (0, part * h, 0))
    panels = [
        add_cores({**parts, **sibling}, pieces[chips[-1], 0])
        for parts, sibling in zip(gathered, siblings)
    ]

    outs = [[] for _ in range(n_col)]
    hold = []
    for k, w in enumerate(thirds):
        source, start = (0, 0) if k == 0 else (1, 0 if k == 1 else thirds[1])
        parts = dict(panels[source])
        if hold:
            parts[(0, 0)] = after(parts[(0, 0)], *hold)
        first = product(gram, parts, start, w)
        first_parts = add_cores(gather_chips(first)[0])
        tile = tiles[source][:, start : start + w]
        result = product(gram, first_parts, 0, w, (tile, first))
        hold = [first_parts[(bit_x, 0)]] + ([] if k == 0 else [last])
        last = result
        back = exchange(result)
        for c in range(n_col):
            outs[c].append(back[c * rows : (c + 1) * rows])
    return jnp.concatenate([piece for out in outs for piece in out], axis=1)


def solution(mesh):
    in_specs = (P(("row", "col"), None),)
    out_specs = P(("row", "col"), None)
    return jax.shard_map(
        per_device, mesh=mesh, in_specs=in_specs, out_specs=out_specs, check_vma=False
    )
```

```python
import functools
import math

import jax
import jax.numpy as jnp
from jax import lax
from jax.experimental import pallas as pl
from jax.experimental.pallas import tpu as pltpu
from jax.sharding import PartitionSpec as P

coef_a = 3.4445
coef_b = -4.775
coef_c = 2.0315
bf16 = jnp.bfloat16
f32 = jnp.float32
VMEM_BYTES = 48 * 1024 * 1024


def widths_of(width, count):
    unit = 256 if width % 256 == 0 else 128
    base, extra = divmod(width // unit, count)
    return [unit * (base + (i >= count - extra)) for i in range(count)]


def dot_t(a, b):
    return lax.dot_general(a, b, (((1,), (1,)), ((), ())), preferred_element_type=f32)


def after(value, *others):
    return lax.optimization_barrier((value, *others))[0]


def swap(value, bit):
    count = lax.axis_size("row")
    return lax.ppermute(value, "row", [(r, r ^ bit) for r in range(count)])


def gather_chips(own):
    count = lax.axis_size("row")
    bit_x, bit_y = count // 4, count // 2
    h = own.shape[0] // 2
    corner = bit_x | bit_y
    parts = {(0, 0): own}
    parts[(bit_x, 0)] = swap(own, bit_x)
    parts[(bit_y, 0)] = swap(own, bit_y)
    from_x, from_y = lax.optimization_barrier((parts[(bit_x, 0)], parts[(bit_y, 0)]))
    upper, lower = lax.optimization_barrier((from_x[:h], from_y[h:]))
    parts[(corner, 0)] = swap(upper, bit_y)
    parts[(corner, h)] = swap(lower, bit_x)
    return parts, (upper, lower)


def add_cores(parts, hold=None):
    bit_x = lax.axis_size("row") // 4
    parts = dict(parts)
    bit = 1
    while bit < bit_x:
        for j, offset in list(parts):
            if (j | bit, offset) not in parts:
                part = parts[(j, offset)]
                if hold is not None:
                    part = after(part, hold)
                parts[(j | bit, offset)] = swap(part, bit)
        bit *= 2
    return parts


def whole_block(parts, j):
    pieces = [parts[key] for key in sorted(parts) if key[0] == j]
    return pieces[0] if len(pieces) == 1 else jnp.concatenate(pieces, axis=0)


def pieces_kernel(count, jobs, scale, low_ref, *refs):
    out = refs[-1]
    h = out.shape[1]

    def product(n, left, right, first):
        total = None
        for k in range(count):
            rows = refs[left * count + k][first : first + h, :]
            term = dot_t(rows, refs[right * count + k][...])
            total = term if total is None else total + term
        out[n] = (total * scale).astype(bf16)

    for n, (left, right, low, first) in enumerate(jobs):
        if low is None:
            product(n, left, right, first)
            continue

        @pl.when(low_ref[low] == 1)
        def _():
            product(n, left, right, 0)

        @pl.when(low_ref[low] == 0)
        def _():
            product(n, right, left, h)


def gram_pieces(blocks, jobs, lows, scale):
    count = len(blocks[0])
    size = blocks[0][0].shape[0]
    width = sum(part.shape[1] for part in blocks[0])
    return pl.pallas_call(
        functools.partial(pieces_kernel, count, jobs, scale),
        out_shape=jax.ShapeDtypeStruct((len(jobs), size // 2, size), bf16),
        in_specs=[pl.BlockSpec(memory_space=pltpu.SMEM)]
        + [pl.BlockSpec(memory_space=pltpu.VMEM)] * (count * len(blocks)),
        out_specs=pl.BlockSpec(memory_space=pltpu.VMEM),
        cost_estimate=pl.CostEstimate(
            flops=len(jobs) * size * size * width,
            bytes_accessed=2 * size * (len(blocks) * width + len(jobs) * size // 2),
            transcendentals=0,
        ),
        compiler_params=pltpu.CompilerParams(vmem_limit_bytes=VMEM_BYTES),
    )(jnp.stack(lows).astype(jnp.int32), *[part for block in blocks for part in block])


def block_kernel(low_ref, mine, theirs, gram_in, out):
    h = mine.shape[0]

    @pl.when(low_ref[0] == 1)
    def _():
        out[:h, :] = mine[...]
        out[h:, :] = theirs[...]

    @pl.when(low_ref[0] == 0)
    def _():
        out[...] = jnp.concatenate([theirs[...], mine[...]], axis=0).T


def put_block(gram, low, mine, theirs, j):
    h, size = mine.shape
    return pl.pallas_call(
        block_kernel,
        grid=(1,),
        out_shape=jax.ShapeDtypeStruct(gram.shape, bf16),
        in_specs=[
            pl.BlockSpec(memory_space=pltpu.SMEM),
            pl.BlockSpec((h, size), lambda i: (0, 0)),
            pl.BlockSpec((h, size), lambda i: (0, 0)),
            pl.BlockSpec(memory_space=pl.ANY),
        ],
        out_specs=pl.BlockSpec((None, size, size), lambda i: (j, 0, 0)),
        input_output_aliases={3: 0},
        cost_estimate=pl.CostEstimate(
            flops=0, bytes_accessed=4 * size * size, transcendentals=0
        ),
        compiler_params=pltpu.CompilerParams(vmem_limit_bytes=VMEM_BYTES),
    )(low, mine, theirs, gram)


def product_kernel(keys, start, finish, me_ref, *refs):
    gram, parts = refs[0], refs[1 : 1 + len(keys)]
    extra = refs[1 + len(keys) : -5]
    out, gbuf, xbuf, acc, sems = refs[-5:]
    count, size, width = xbuf.shape
    h = size // 2

    def piece(j, part):
        return xbuf.at[j, pl.ds(part * h, h)], sems.at[j, part]

    copies = []
    for j in range(count):
        copies.append(pltpu.make_async_copy(gram.at[j], gbuf.at[j], sems.at[j, 2]))
        for part in range(2):
            if keys[0] is None:
                first = pl.multiple_of((me_ref[0] ^ j) * size + part * h, 16)
                source = parts[0].at[pl.ds(first, h), pl.ds(start, width)]
            else:
                key = (j, part * h) if (j, part * h) in keys else (j, 0)
                first = part * h - key[1]
                source = parts[keys.index(key)].at[pl.ds(first, h), pl.ds(start, width)]
            copies.append(pltpu.make_async_copy(source, *piece(j, part)))
    for copy in copies:
        copy.start()
    acc[...] = jnp.zeros_like(acc)

    @pl.loop(0, count)
    def _(j):
        pltpu.make_async_copy(gbuf.at[j], gbuf.at[j], sems.at[j, 2]).wait()
        for part in range(2):
            there, sem = piece(j, part)
            pltpu.make_async_copy(there, there, sem).wait()
        acc[...] += jnp.dot(gbuf[j], xbuf[j], preferred_element_type=f32)

    if finish:
        tile, first = extra
        out[...] = (
            coef_a * tile[...].astype(f32)
            + coef_b * first[...].astype(f32)
            + coef_c * acc[...]
        ).astype(bf16)
    else:
        out[...] = acc[...].astype(bf16)


def product(gram, me, parts, start, width, extra=()):
    count, size, _ = gram.shape
    keys = sorted(parts)
    flops = 2 * count * size * size * width
    return pl.pallas_call(
        functools.partial(product_kernel, keys, start, bool(extra)),
        out_shape=jax.ShapeDtypeStruct((size, width), bf16),
        in_specs=[pl.BlockSpec(memory_space=pltpu.SMEM)]
        + [pl.BlockSpec(memory_space=pl.ANY)] * (1 + len(keys))
        + [pl.BlockSpec(memory_space=pltpu.VMEM)] * len(extra),
        out_specs=pl.BlockSpec(memory_space=pltpu.VMEM),
        scratch_shapes=[
            pltpu.VMEM((count, size, size), bf16),
            pltpu.VMEM((count, size, width), bf16),
            pltpu.VMEM((size, width), f32),
            pltpu.SemaphoreType.DMA((count, 3)),
        ],
        cost_estimate=pl.CostEstimate(
            flops=flops,
            bytes_accessed=2 * count * size * (size + width),
            transcendentals=0,
        ),
        compiler_params=pltpu.CompilerParams(vmem_limit_bytes=VMEM_BYTES),
    )(me.astype(jnp.int32).reshape(1), gram, *[parts[key] for key in keys], *extra)


def per_device(ortho_in):
    rows, cols = ortho_in.shape
    n_row = lax.axis_size("row")
    n_col = lax.axis_size("col")
    me = lax.axis_index("row")
    block = rows * n_col
    width = cols // n_col
    scale = 1.0 / (math.sqrt(block * n_row) + math.sqrt(cols)) ** 2
    h = block // 2
    bit_x, bit_y = n_row // 4, n_row // 2
    cores = range(1, bit_x)
    chips = (bit_x, bit_y, bit_x | bit_y)

    def exchange(value):
        return lax.all_to_all(value, "col", split_axis=0, concat_axis=0, tiled=True)

    tiles, gathered, siblings, tied = [], [], [], []
    start = 0
    thirds = widths_of(width, 3)
    for k, w in enumerate(thirds):
        first = [start + c * width for c in range(n_col)]
        part = jnp.concatenate([ortho_in[:, f : f + w] for f in first], axis=0)
        if k == 2:
            part = after(part, gathered[0][(bit_x, 0)], gathered[0][(bit_y, 0)])
        tile = exchange(part)
        tiles.append(tile)
        parts, tie = gather_chips(tile)
        gathered.append(parts)
        tied.extend(tie)
        siblings.append(add_cores({(0, 0): tile}))
        start += w

    def low_of(j):
        return ((me & (1 << (j.bit_length() - 1))) == 0).astype(jnp.int32).reshape(1)

    gram = jnp.zeros((n_row, block, block), bf16)
    lefts = [[s[(i, 0)] for s in siblings] for i in range(bit_x)]
    jobs = [(0, 0, None, 0), (0, 0, None, h)] + [(0, j, j - 1, 0) for j in cores]
    near = gram_pieces(lefts, jobs, [low_of(j)[0] for j in cores], scale)
    last = near = lax.psum(near, "col")
    gram = lax.dynamic_update_slice(gram, near[:2].reshape(1, block, block), (0, 0, 0))
    for j in cores:
        gram = put_block(gram, low_of(j), near[1 + j], swap(near[1 + j], j), j)
    for stage in (chips[:2], chips[2:]):
        blocks = list(lefts)
        for j in stage:
            peers = [whole_block(parts, j) for parts in gathered]
            if j != chips[-1]:
                peers[0] = after(peers[0], *tied)
            blocks.append(peers)
        jobs = [(i, bit_x + n, n, 0) for n in range(len(stage)) for i in range(bit_x)]
        pieces = gram_pieces(blocks, jobs, [low_of(j)[0] for j in stage], scale)
        last = sums = lax.psum(after(pieces, last), "col")
        for n, j in enumerate(stage):
            for i in range(bit_x):
                mine = sums[n * bit_x + i]
                theirs = swap(mine, j)
                if i > 0:
                    mine = swap(mine, i)
                gram = put_block(gram, low_of(j), mine, theirs, j | i)
    panels = [
        add_cores({**parts, **sibling}) for parts, sibling in zip(gathered, siblings)
    ]

    outs = [[] for _ in range(n_col)]
    for k, w in enumerate(thirds):
        first = product(gram, me, panels[k], 0, w)
        first_panel = lax.all_gather(first, "row", axis=0, tiled=True)
        result = product(gram, me, {None: first_panel}, 0, w, (tiles[k], first))
        back = exchange(result)
        for c in range(n_col):
            outs[c].append(back[c * rows : (c + 1) * rows])
    return jnp.concatenate([piece for out in outs for piece in out], axis=1)


def solution(mesh):
    in_specs = (P(("row", "col"), None),)
    out_specs = P(("row", "col"), None)
    return jax.shard_map(
        per_device, mesh=mesh, in_specs=in_specs, out_specs=out_specs, check_vma=False
    )
```

```python
import functools
import math

import jax
import jax.numpy as jnp
from jax import lax
from jax.experimental import pallas as pl
from jax.experimental.pallas import tpu as pltpu
from jax.sharding import PartitionSpec as P

coef_a = 3.4445
coef_b = -4.775
coef_c = 2.0315
bf16 = jnp.bfloat16
f32 = jnp.float32
VMEM_BYTES = 48 * 1024 * 1024


def widths_of(width, count):
    unit = 256 if width % 256 == 0 else 128
    base, extra = divmod(width // unit, count)
    return [unit * (base + (i >= count - extra)) for i in range(count)]


def dot_t(a, b):
    return lax.dot_general(a, b, (((1,), (1,)), ((), ())), preferred_element_type=f32)


def after(value, *others):
    return lax.optimization_barrier((value, *others))[0]


def swap(value, bit):
    count = lax.axis_size("row")
    return lax.ppermute(value, "row", [(r, r ^ bit) for r in range(count)])


def gather_chips(own):
    count = lax.axis_size("row")
    bit_x, bit_y = count // 4, count // 2
    h = own.shape[0] // 2
    corner = bit_x | bit_y
    parts = {(0, 0): own}
    parts[(bit_x, 0)] = swap(own, bit_x)
    parts[(bit_y, 0)] = swap(own, bit_y)
    from_x, from_y = lax.optimization_barrier((parts[(bit_x, 0)], parts[(bit_y, 0)]))
    upper, lower = lax.optimization_barrier((from_x[:h], from_y[h:]))
    parts[(corner, 0)] = swap(upper, bit_y)
    parts[(corner, h)] = swap(lower, bit_x)
    return parts, (upper, lower)


def add_cores(parts, hold=None):
    bit_x = lax.axis_size("row") // 4
    parts = dict(parts)
    bit = 1
    while bit < bit_x:
        for j, offset in list(parts):
            if (j | bit, offset) not in parts:
                part = parts[(j, offset)]
                if hold is not None:
                    part = after(part, hold)
                parts[(j | bit, offset)] = swap(part, bit)
        bit *= 2
    return parts


def whole_block(parts, j):
    pieces = [parts[key] for key in sorted(parts) if key[0] == j]
    return pieces[0] if len(pieces) == 1 else jnp.concatenate(pieces, axis=0)


def pieces_kernel(count, jobs, scale, low_ref, *refs):
    out = refs[-1]
    h = out.shape[1]

    def product(n, left, right, first):
        total = None
        for k in range(count):
            rows = refs[left * count + k][first : first + h, :]
            term = dot_t(rows, refs[right * count + k][...])
            total = term if total is None else total + term
        out[n] = (total * scale).astype(bf16)

    for n, (left, right, low, first) in enumerate(jobs):
        if low is None:
            product(n, left, right, first)
            continue

        @pl.when(low_ref[low] == 1)
        def _():
            product(n, left, right, 0)

        @pl.when(low_ref[low] == 0)
        def _():
            product(n, right, left, h)


def gram_pieces(blocks, jobs, lows, scale):
    count = len(blocks[0])
    size = blocks[0][0].shape[0]
    width = sum(part.shape[1] for part in blocks[0])
    return pl.pallas_call(
        functools.partial(pieces_kernel, count, jobs, scale),
        out_shape=jax.ShapeDtypeStruct((len(jobs), size // 2, size), bf16),
        in_specs=[pl.BlockSpec(memory_space=pltpu.SMEM)]
        + [pl.BlockSpec(memory_space=pltpu.VMEM)] * (count * len(blocks)),
        out_specs=pl.BlockSpec(memory_space=pltpu.VMEM),
        cost_estimate=pl.CostEstimate(
            flops=len(jobs) * size * size * width,
            bytes_accessed=2 * size * (len(blocks) * width + len(jobs) * size // 2),
            transcendentals=0,
        ),
        compiler_params=pltpu.CompilerParams(vmem_limit_bytes=VMEM_BYTES),
    )(jnp.stack(lows).astype(jnp.int32), *[part for block in blocks for part in block])


def block_kernel(low_ref, mine, theirs, gram_in, out):
    h = mine.shape[0]

    @pl.when(low_ref[0] == 1)
    def _():
        out[:h, :] = mine[...]
        out[h:, :] = theirs[...]

    @pl.when(low_ref[0] == 0)
    def _():
        out[...] = jnp.concatenate([theirs[...], mine[...]], axis=0).T


def put_block(gram, low, mine, theirs, j):
    h, size = mine.shape
    return pl.pallas_call(
        block_kernel,
        grid=(1,),
        out_shape=jax.ShapeDtypeStruct(gram.shape, bf16),
        in_specs=[
            pl.BlockSpec(memory_space=pltpu.SMEM),
            pl.BlockSpec((h, size), lambda i: (0, 0)),
            pl.BlockSpec((h, size), lambda i: (0, 0)),
            pl.BlockSpec(memory_space=pl.ANY),
        ],
        out_specs=pl.BlockSpec((None, size, size), lambda i: (j, 0, 0)),
        input_output_aliases={3: 0},
        cost_estimate=pl.CostEstimate(
            flops=0, bytes_accessed=4 * size * size, transcendentals=0
        ),
        compiler_params=pltpu.CompilerParams(vmem_limit_bytes=VMEM_BYTES),
    )(low, mine, theirs, gram)


def product_kernel(keys, start, finish, me_ref, *refs):
    gram, parts = refs[0], refs[1 : 1 + len(keys)]
    extra = refs[1 + len(keys) : -5]
    out, gbuf, xbuf, acc, sems = refs[-5:]
    count, size, width = xbuf.shape
    h = size // 2

    def piece(j, part):
        return xbuf.at[j, pl.ds(part * h, h)], sems.at[j, part]

    copies = []
    for j in range(count):
        copies.append(pltpu.make_async_copy(gram.at[j], gbuf.at[j], sems.at[j, 2]))
        for part in range(2):
            if keys[0] is None:
                first = pl.multiple_of((me_ref[0] ^ j) * size + part * h, 16)
                source = parts[0].at[pl.ds(first, h), pl.ds(start, width)]
            else:
                key = (j, part * h) if (j, part * h) in keys else (j, 0)
                first = part * h - key[1]
                source = parts[keys.index(key)].at[pl.ds(first, h), pl.ds(start, width)]
            copies.append(pltpu.make_async_copy(source, *piece(j, part)))
    for copy in copies:
        copy.start()
    acc[...] = jnp.zeros_like(acc)

    @pl.loop(0, count)
    def _(j):
        pltpu.make_async_copy(gbuf.at[j], gbuf.at[j], sems.at[j, 2]).wait()
        for part in range(2):
            there, sem = piece(j, part)
            pltpu.make_async_copy(there, there, sem).wait()
        acc[...] += jnp.dot(gbuf[j], xbuf[j], preferred_element_type=f32)

    if finish:
        tile, first = extra
        out[...] = (
            coef_a * tile[...].astype(f32)
            + coef_b * first[...].astype(f32)
            + coef_c * acc[...]
        ).astype(bf16)
    else:
        out[...] = acc[...].astype(bf16)


def product(gram, me, parts, start, width, extra=()):
    count, size, _ = gram.shape
    keys = sorted(parts)
    flops = 2 * count * size * size * width
    return pl.pallas_call(
        functools.partial(product_kernel, keys, start, bool(extra)),
        out_shape=jax.ShapeDtypeStruct((size, width), bf16),
        in_specs=[pl.BlockSpec(memory_space=pltpu.SMEM)]
        + [pl.BlockSpec(memory_space=pl.ANY)] * (1 + len(keys))
        + [pl.BlockSpec(memory_space=pltpu.VMEM)] * len(extra),
        out_specs=pl.BlockSpec(memory_space=pltpu.VMEM),
        scratch_shapes=[
            pltpu.VMEM((count, size, size), bf16),
            pltpu.VMEM((count, size, width), bf16),
            pltpu.VMEM((size, width), f32),
            pltpu.SemaphoreType.DMA((count, 3)),
        ],
        cost_estimate=pl.CostEstimate(
            flops=flops,
            bytes_accessed=2 * count * size * (size + width),
            transcendentals=0,
        ),
        compiler_params=pltpu.CompilerParams(vmem_limit_bytes=VMEM_BYTES),
    )(me.astype(jnp.int32).reshape(1), gram, *[parts[key] for key in keys], *extra)


def sum_on_line(piece, arrivals):
    count = lax.axis_size("col")
    me = lax.axis_index("col")
    half = count // 2

    def send(stage, value, pairs):
        done = arrivals.setdefault(stage, [])
        if len(done) > 1:
            value = after(value, done[-2])
        arrived = lax.ppermute(value, "col", pairs)
        done.append(arrived)
        return arrived

    def add(left, right):
        return (left.astype(f32) + right.astype(f32)).astype(bf16)

    for s in range(half - 1):
        pairs = [(s, s + 1), (count - 1 - s, count - 2 - s)]
        piece = add(piece, send(s, piece, pairs))
    piece = add(piece, send(half - 1, piece, [(half - 1, half), (half, half - 1)]))
    for s in range(half - 2, -1, -1):
        pairs = [(s + 1, s), (count - 2 - s, count - 1 - s)]
        arrived = send(2 * half - 2 - s, piece, pairs)
        piece = jnp.where((me == s) | (me == count - 1 - s), arrived, piece)
    return piece


def per_device(ortho_in):
    rows, cols = ortho_in.shape
    n_row = lax.axis_size("row")
    n_col = lax.axis_size("col")
    me = lax.axis_index("row")
    block = rows * n_col
    width = cols // n_col
    scale = 1.0 / (math.sqrt(block * n_row) + math.sqrt(cols)) ** 2
    h = block // 2
    bit_x, bit_y = n_row // 4, n_row // 2
    cores = range(1, bit_x)
    chips = (bit_x, bit_y, bit_x | bit_y)

    def exchange(value):
        return lax.all_to_all(value, "col", split_axis=0, concat_axis=0, tiled=True)

    tiles, gathered, siblings, tied = [], [], [], []
    start = 0
    thirds = widths_of(width, 3)
    for k, w in enumerate(thirds):
        first = [start + c * width for c in range(n_col)]
        part = jnp.concatenate([ortho_in[:, f : f + w] for f in first], axis=0)
        if k == 2:
            part = after(part, gathered[0][(bit_x, 0)], gathered[0][(bit_y, 0)])
        tile = exchange(part)
        tiles.append(tile)
        parts, tie = gather_chips(tile)
        gathered.append(parts)
        tied.extend(tie)
        siblings.append(add_cores({(0, 0): tile}))
        start += w

    def low_of(j):
        return ((me & (1 << (j.bit_length() - 1))) == 0).astype(jnp.int32).reshape(1)

    lefts = [[s[(i, 0)] for s in siblings] for i in range(bit_x)]
    arrivals = {}

    def on_line(pieces):
        return [sum_on_line(pieces[n], arrivals) for n in range(pieces.shape[0])]

    own = gram_pieces(lefts[:1], [(0, 0, None, 0), (0, 0, None, h)], [me], scale)
    own = last = lax.psum(own, "col")
    sums = {}
    jobs = [(0, j, j - 1, 0) for j in cores]
    near = gram_pieces(lefts, jobs, [low_of(j)[0] for j in cores], scale)
    for j, piece in zip(cores, on_line(near)):
        sums[j, 0] = piece
    for j in chips:
        peers = [whole_block(parts, j) for parts in gathered]
        if j != chips[-1]:
            peers[0] = after(peers[0], *tied, gathered[0][(chips[-1], 0)])
        jobs = [(i, bit_x, 0, 0) for i in range(bit_x)]
        if j == chips[-1]:
            parts = [
                gram_pieces(lefts + [peers], jobs[:1], [low_of(j)[0]], scale),
                gram_pieces(lefts + [peers], jobs[1:], [low_of(j)[0]], scale),
            ]
            head = last = lax.psum(after(parts[0], last), "col")
            total = [head[0]] + on_line(parts[1])
        else:
            pieces = gram_pieces(lefts + [peers], jobs, [low_of(j)[0]], scale)
            if j == bit_x:
                total = last = lax.psum(after(pieces, last), "col")
            else:
                total = on_line(pieces)
        for i in range(bit_x):
            sums[j, i] = total[i]
    gram = lax.dynamic_update_slice(
        jnp.zeros((n_row, block, block), bf16), own.reshape(1, block, block), (0, 0, 0)
    )
    for (j, i), mine in sums.items():
        theirs = swap(mine, j)
        if i > 0:
            mine = swap(mine, i)
        gram = put_block(gram, low_of(j), mine, theirs, j | i)
    panels = [
        add_cores({**parts, **sibling}) for parts, sibling in zip(gathered, siblings)
    ]

    outs = []
    for k, w in enumerate(thirds):
        first = product(gram, me, panels[k], 0, w)
        if k == 1:
            first_parts = add_cores(gather_chips(first)[0])
        else:
            first_parts = {None: lax.all_gather(first, "row", axis=0, tiled=True)}
        result = product(gram, me, first_parts, 0, w, (tiles[k], first))
        back = lax.all_to_all(result, "col", split_axis=0, concat_axis=1, tiled=True)
        outs.append(back.reshape(rows, n_col, w))
    return jnp.concatenate(outs, axis=2).reshape(rows, cols)


def solution(mesh):
    in_specs = (P(("row", "col"), None),)
    out_specs = P(("row", "col"), None)
    return jax.shard_map(
        per_device, mesh=mesh, in_specs=in_specs, out_specs=out_specs, check_vma=False
    )
```

```python
import functools
import math

import jax
import jax.numpy as jnp
from jax import lax
from jax.experimental import pallas as pl
from jax.experimental.pallas import tpu as pltpu
from jax.sharding import PartitionSpec as P

coef_a = 3.4445
coef_b = -4.775
coef_c = 2.0315
bf16 = jnp.bfloat16
f32 = jnp.float32
VMEM_BYTES = 48 * 1024 * 1024


def widths_of(width, count):
    unit = 256 if width % 256 == 0 else 128
    base, extra = divmod(width // unit, count)
    return [unit * (base + (i >= count - extra)) for i in range(count)]


def dot_t(a, b):
    return lax.dot_general(a, b, (((1,), (1,)), ((), ())), preferred_element_type=f32)


def after(value, *others):
    return lax.optimization_barrier((value, *others))[0]


def swap(value, bit):
    count = lax.axis_size("row")
    return lax.ppermute(value, "row", [(r, r ^ bit) for r in range(count)])


def gather_chips(own):
    count = lax.axis_size("row")
    bit_x, bit_y = count // 4, count // 2
    h = own.shape[0] // 2
    corner = bit_x | bit_y
    parts = {(0, 0): own}
    parts[(bit_x, 0)] = swap(own, bit_x)
    parts[(bit_y, 0)] = swap(own, bit_y)
    from_x, from_y = lax.optimization_barrier((parts[(bit_x, 0)], parts[(bit_y, 0)]))
    upper, lower = lax.optimization_barrier((from_x[:h], from_y[h:]))
    parts[(corner, 0)] = swap(upper, bit_y)
    parts[(corner, h)] = swap(lower, bit_x)
    return parts, (upper, lower)


def add_cores(parts, hold=None):
    bit_x = lax.axis_size("row") // 4
    parts = dict(parts)
    bit = 1
    while bit < bit_x:
        for j, offset in list(parts):
            if (j | bit, offset) not in parts:
                part = parts[(j, offset)]
                if hold is not None:
                    part = after(part, hold)
                parts[(j | bit, offset)] = swap(part, bit)
        bit *= 2
    return parts


def whole_block(parts, j):
    pieces = [parts[key] for key in sorted(parts) if key[0] == j]
    return pieces[0] if len(pieces) == 1 else jnp.concatenate(pieces, axis=0)


def pieces_kernel(count, jobs, scale, low_ref, *refs):
    out = refs[-1]
    h = out.shape[1]

    def product(n, left, right, first):
        total = None
        for k in range(count):
            rows = refs[left * count + k][first : first + h, :]
            term = dot_t(rows, refs[right * count + k][...])
            total = term if total is None else total + term
        out[n] = (total * scale).astype(bf16)

    for n, (left, right, low, first) in enumerate(jobs):
        if low is None:
            product(n, left, right, first)
            continue

        @pl.when(low_ref[low] == 1)
        def _():
            product(n, left, right, 0)

        @pl.when(low_ref[low] == 0)
        def _():
            product(n, right, left, h)


def gram_pieces(blocks, jobs, lows, scale):
    count = len(blocks[0])
    size = blocks[0][0].shape[0]
    width = sum(part.shape[1] for part in blocks[0])
    return pl.pallas_call(
        functools.partial(pieces_kernel, count, jobs, scale),
        out_shape=jax.ShapeDtypeStruct((len(jobs), size // 2, size), bf16),
        in_specs=[pl.BlockSpec(memory_space=pltpu.SMEM)]
        + [pl.BlockSpec(memory_space=pltpu.VMEM)] * (count * len(blocks)),
        out_specs=pl.BlockSpec(memory_space=pltpu.VMEM),
        cost_estimate=pl.CostEstimate(
            flops=len(jobs) * size * size * width,
            bytes_accessed=2 * size * (len(blocks) * width + len(jobs) * size // 2),
            transcendentals=0,
        ),
        compiler_params=pltpu.CompilerParams(vmem_limit_bytes=VMEM_BYTES),
    )(jnp.stack(lows).astype(jnp.int32), *[part for block in blocks for part in block])


def block_kernel(low_ref, mine, theirs, gram_in, out):
    h = mine.shape[0]

    @pl.when(low_ref[0] == 1)
    def _():
        out[:h, :] = mine[...]
        out[h:, :] = theirs[...]

    @pl.when(low_ref[0] == 0)
    def _():
        out[...] = jnp.concatenate([theirs[...], mine[...]], axis=0).T


def put_block(gram, low, mine, theirs, j):
    (mine, m), (theirs, t) = mine, theirs
    _, h, size = mine.shape
    return pl.pallas_call(
        block_kernel,
        grid=(1,),
        out_shape=jax.ShapeDtypeStruct(gram.shape, bf16),
        in_specs=[
            pl.BlockSpec(memory_space=pltpu.SMEM),
            pl.BlockSpec((None, h, size), lambda i: (m, 0, 0)),
            pl.BlockSpec((None, h, size), lambda i: (t, 0, 0)),
            pl.BlockSpec(memory_space=pl.ANY),
        ],
        out_specs=pl.BlockSpec((None, size, size), lambda i: (j, 0, 0)),
        input_output_aliases={3: 0},
        cost_estimate=pl.CostEstimate(
            flops=0, bytes_accessed=4 * size * size, transcendentals=0
        ),
        compiler_params=pltpu.CompilerParams(vmem_limit_bytes=VMEM_BYTES),
    )(low, mine, theirs, gram)


def own_kernel(halves, out):
    h = halves.shape[1]
    out[:h, :] = halves[0]
    out[h:, :] = halves[1]


def start_gram(halves, count):
    _, h, size = halves.shape
    return pl.pallas_call(
        own_kernel,
        grid=(1,),
        out_shape=jax.ShapeDtypeStruct((count, size, size), bf16),
        in_specs=[pl.BlockSpec((2, h, size), lambda i: (0, 0, 0))],
        out_specs=pl.BlockSpec((None, size, size), lambda i: (0, 0, 0)),
        cost_estimate=pl.CostEstimate(
            flops=0, bytes_accessed=4 * size * size, transcendentals=0
        ),
        compiler_params=pltpu.CompilerParams(vmem_limit_bytes=VMEM_BYTES),
    )(halves)


def product_kernel(keys, start, finish, me_ref, *refs):
    gram, parts = refs[0], refs[1 : 1 + len(keys)]
    extra = refs[1 + len(keys) : -5]
    out, gbuf, xbuf, acc, sems = refs[-5:]
    count, size, width = xbuf.shape
    h = size // 2

    def piece(j, part):
        return xbuf.at[j, pl.ds(part * h, h)], sems.at[j, part]

    copies = []
    for j in range(count):
        copies.append(pltpu.make_async_copy(gram.at[j], gbuf.at[j], sems.at[j, 2]))
        for part in range(2):
            if keys[0] is None:
                first = pl.multiple_of((me_ref[0] ^ j) * size + part * h, 16)
                source = parts[0].at[pl.ds(first, h), pl.ds(start, width)]
            else:
                key = (j, part * h) if (j, part * h) in keys else (j, 0)
                first = part * h - key[1]
                source = parts[keys.index(key)].at[pl.ds(first, h), pl.ds(start, width)]
            copies.append(pltpu.make_async_copy(source, *piece(j, part)))
    for copy in copies:
        copy.start()
    acc[...] = jnp.zeros_like(acc)

    @pl.loop(0, count)
    def _(j):
        pltpu.make_async_copy(gbuf.at[j], gbuf.at[j], sems.at[j, 2]).wait()
        for part in range(2):
            there, sem = piece(j, part)
            pltpu.make_async_copy(there, there, sem).wait()
        acc[...] += jnp.dot(gbuf[j], xbuf[j], preferred_element_type=f32)

    if finish:
        tile, first = extra
        out[...] = (
            coef_a * tile[...].astype(f32)
            + coef_b * first[...].astype(f32)
            + coef_c * acc[...]
        ).astype(bf16)
    else:
        out[...] = acc[...].astype(bf16)


def product(gram, me, parts, start, width, extra=()):
    count, size, _ = gram.shape
    keys = sorted(parts)
    flops = 2 * count * size * size * width
    return pl.pallas_call(
        functools.partial(product_kernel, keys, start, bool(extra)),
        out_shape=jax.ShapeDtypeStruct((size, width), bf16),
        in_specs=[pl.BlockSpec(memory_space=pltpu.SMEM)]
        + [pl.BlockSpec(memory_space=pl.ANY)] * (1 + len(keys))
        + [pl.BlockSpec(memory_space=pltpu.VMEM)] * len(extra),
        out_specs=pl.BlockSpec(memory_space=pltpu.VMEM),
        scratch_shapes=[
            pltpu.VMEM((count, size, size), bf16),
            pltpu.VMEM((count, size, width), bf16),
            pltpu.VMEM((size, width), f32),
            pltpu.SemaphoreType.DMA((count, 3)),
        ],
        cost_estimate=pl.CostEstimate(
            flops=flops,
            bytes_accessed=2 * count * size * (size + width),
            transcendentals=0,
        ),
        compiler_params=pltpu.CompilerParams(vmem_limit_bytes=VMEM_BYTES),
    )(me.astype(jnp.int32).reshape(1), gram, *[parts[key] for key in keys], *extra)


def per_device(ortho_in):
    rows, cols = ortho_in.shape
    n_row = lax.axis_size("row")
    n_col = lax.axis_size("col")
    me = lax.axis_index("row")
    block = rows * n_col
    width = cols // n_col
    scale = 1.0 / (math.sqrt(block * n_row) + math.sqrt(cols)) ** 2
    h = block // 2
    bit_x, bit_y = n_row // 4, n_row // 2
    cores = range(1, bit_x)
    chips = (bit_x, bit_y, bit_x | bit_y)

    def exchange(value):
        return lax.all_to_all(value, "col", split_axis=0, concat_axis=0, tiled=True)

    tiles, gathered, siblings, tied = [], [], [], []
    start = 0
    thirds = widths_of(width, 3)
    if width % (9 * 256) == 0:
        thirds = [width // 9 * n for n in (3, 4, 2)]
    for k, w in enumerate(thirds):
        first = [start + c * width for c in range(n_col)]
        part = jnp.concatenate([ortho_in[:, f : f + w] for f in first], axis=0)
        if k == 2:
            part = after(part, gathered[0][(bit_x, 0)], gathered[0][(bit_y, 0)])
        tile = exchange(part)
        tiles.append(tile)
        parts, tie = gather_chips(tile)
        gathered.append(parts)
        tied.extend(tie)
        siblings.append(add_cores({(0, 0): tile}))
        start += w

    def low_of(j):
        return ((me & (1 << (j.bit_length() - 1))) == 0).astype(jnp.int32).reshape(1)

    lefts = [[s[(i, 0)] for s in siblings] for i in range(bit_x)]
    jobs = [(0, 0, None, 0), (0, 0, None, h)] + [(0, j, j - 1, 0) for j in cores]
    near = gram_pieces(lefts, jobs, [low_of(j)[0] for j in cores], scale)
    last = near = lax.psum(near, "col")
    gram = start_gram(near, n_row)
    for j in cores:
        theirs = swap(near[1 + j : 2 + j], j)
        gram = put_block(gram, low_of(j), (near, 1 + j), (theirs, 0), j)
    panels = [
        add_cores({**parts, **sibling}) for parts, sibling in zip(gathered, siblings)
    ]
    for stage in (chips[:2], chips[2:]):
        blocks = list(lefts)
        for j in stage:
            peers = [whole_block(parts, j) for parts in gathered]
            if j != chips[-1]:
                peers[0] = after(peers[0], *tied)
            blocks.append(peers)
        jobs = [(i, bit_x + n, n, 0) for n in range(len(stage)) for i in range(bit_x)]
        pieces = gram_pieces(blocks, jobs, [low_of(j)[0] for j in stage], scale)
        held = list(panels[0].values()) if len(stage) == 1 else []
        last = sums = lax.psum(after(pieces, last, *held), "col")
        for n, j in enumerate(stage):
            theirs = swap(sums[n * bit_x : (n + 1) * bit_x], j)
            gram = put_block(gram, low_of(j), (sums, n * bit_x), (theirs, 0), j)
            for i in cores:
                mine = swap(sums[n * bit_x + i : n * bit_x + i + 1], i)
                gram = put_block(gram, low_of(j), (mine, 0), (theirs, i), j | i)

    outs = []
    for k, w in enumerate(thirds):
        first = product(gram, me, panels[k], 0, w)
        first_panel = lax.all_gather(first, "row", axis=0, tiled=True)
        result = product(gram, me, {None: first_panel}, 0, w, (tiles[k], first))
        back = lax.all_to_all(result, "col", split_axis=0, concat_axis=1, tiled=True)
        outs.append(back.reshape(rows, n_col, w))
    return jnp.concatenate(outs, axis=2).reshape(rows, cols)


def solution(mesh):
    in_specs = (P(("row", "col"), None),)
    out_specs = P(("row", "col"), None)
    return jax.shard_map(
        per_device, mesh=mesh, in_specs=in_specs, out_specs=out_specs, check_vma=False
    )
```

```python
import functools
import math

import jax
import jax.numpy as jnp
from jax import lax
from jax.experimental import pallas as pl
from jax.experimental.pallas import tpu as pltpu
from jax.sharding import PartitionSpec as P

coef_a = 3.4445
coef_b = -4.775
coef_c = 2.0315
bf16 = jnp.bfloat16
f32 = jnp.float32
VMEM_BYTES = 48 * 1024 * 1024


def widths_of(width, count):
    unit = 256 if width % 256 == 0 else 128
    base, extra = divmod(width // unit, count)
    return [unit * (base + (i >= count - extra)) for i in range(count)]


def dot_t(a, b):
    return lax.dot_general(a, b, (((1,), (1,)), ((), ())), preferred_element_type=f32)


def after(value, *others):
    return lax.optimization_barrier((value, *others))[0]


def swap(value, bit):
    count = lax.axis_size("row")
    return lax.ppermute(value, "row", [(r, r ^ bit) for r in range(count)])


def gather_chips(own):
    count = lax.axis_size("row")
    bit_x, bit_y = count // 4, count // 2
    h = own.shape[0] // 2
    corner = bit_x | bit_y
    parts = {(0, 0): own}
    parts[(bit_x, 0)] = swap(own, bit_x)
    parts[(bit_y, 0)] = swap(own, bit_y)
    from_x, from_y = lax.optimization_barrier((parts[(bit_x, 0)], parts[(bit_y, 0)]))
    upper, lower = lax.optimization_barrier((from_x[:h], from_y[h:]))
    parts[(corner, 0)] = swap(upper, bit_y)
    parts[(corner, h)] = swap(lower, bit_x)
    return parts, (upper, lower)


def add_cores(parts, hold=None):
    bit_x = lax.axis_size("row") // 4
    parts = dict(parts)
    bit = 1
    while bit < bit_x:
        for j, offset in list(parts):
            if (j | bit, offset) not in parts:
                part = parts[(j, offset)]
                if hold is not None:
                    part = after(part, hold)
                parts[(j | bit, offset)] = swap(part, bit)
        bit *= 2
    return parts


def whole_block(parts, j):
    pieces = [parts[key] for key in sorted(parts) if key[0] == j]
    return pieces[0] if len(pieces) == 1 else jnp.concatenate(pieces, axis=0)


def pieces_kernel(count, jobs, scale, low_ref, *refs):
    out = refs[-1]
    h = out.shape[1]

    def product(n, left, right, first):
        total = None
        for k in range(count):
            rows = refs[left * count + k][first : first + h, :]
            term = dot_t(rows, refs[right * count + k][...])
            total = term if total is None else total + term
        out[n] = (total * scale).astype(bf16)

    for n, (left, right, low, first) in enumerate(jobs):
        if low is None:
            product(n, left, right, first)
            continue

        @pl.when(low_ref[low] == 1)
        def _():
            product(n, left, right, 0)

        @pl.when(low_ref[low] == 0)
        def _():
            product(n, right, left, h)


def gram_pieces(blocks, jobs, lows, scale):
    count = len(blocks[0])
    size = blocks[0][0].shape[0]
    width = sum(part.shape[1] for part in blocks[0])
    return pl.pallas_call(
        functools.partial(pieces_kernel, count, jobs, scale),
        out_shape=jax.ShapeDtypeStruct((len(jobs), size // 2, size), bf16),
        in_specs=[pl.BlockSpec(memory_space=pltpu.SMEM)]
        + [pl.BlockSpec(memory_space=pltpu.VMEM)] * (count * len(blocks)),
        out_specs=pl.BlockSpec(memory_space=pltpu.VMEM),
        cost_estimate=pl.CostEstimate(
            flops=len(jobs) * size * size * width,
            bytes_accessed=2 * size * (len(blocks) * width + len(jobs) * size // 2),
            transcendentals=0,
        ),
        compiler_params=pltpu.CompilerParams(vmem_limit_bytes=VMEM_BYTES),
    )(jnp.stack(lows).astype(jnp.int32), *[part for block in blocks for part in block])


def block_kernel(low_ref, mine, theirs, gram_in, out):
    h = mine.shape[0]

    @pl.when(low_ref[0] == 1)
    def _():
        out[:h, :] = mine[...]
        out[h:, :] = theirs[...]

    @pl.when(low_ref[0] == 0)
    def _():
        out[...] = jnp.concatenate([theirs[...], mine[...]], axis=0).T


def put_block(gram, low, mine, theirs, j):
    (mine, m), (theirs, t) = mine, theirs
    _, h, size = mine.shape
    return pl.pallas_call(
        block_kernel,
        grid=(1,),
        out_shape=jax.ShapeDtypeStruct(gram.shape, bf16),
        in_specs=[
            pl.BlockSpec(memory_space=pltpu.SMEM),
            pl.BlockSpec((None, h, size), lambda i: (m, 0, 0)),
            pl.BlockSpec((None, h, size), lambda i: (t, 0, 0)),
            pl.BlockSpec(memory_space=pl.ANY),
        ],
        out_specs=pl.BlockSpec((None, size, size), lambda i: (j, 0, 0)),
        input_output_aliases={3: 0},
        cost_estimate=pl.CostEstimate(
            flops=0, bytes_accessed=4 * size * size, transcendentals=0
        ),
        compiler_params=pltpu.CompilerParams(vmem_limit_bytes=VMEM_BYTES),
    )(low, mine, theirs, gram)


def own_kernel(halves, out):
    h = halves.shape[1]
    out[:h, :] = halves[0]
    out[h:, :] = halves[1]


def start_gram(halves, count):
    _, h, size = halves.shape
    return pl.pallas_call(
        own_kernel,
        grid=(1,),
        out_shape=jax.ShapeDtypeStruct((count, size, size), bf16),
        in_specs=[pl.BlockSpec((2, h, size), lambda i: (0, 0, 0))],
        out_specs=pl.BlockSpec((None, size, size), lambda i: (0, 0, 0)),
        cost_estimate=pl.CostEstimate(
            flops=0, bytes_accessed=4 * size * size, transcendentals=0
        ),
        compiler_params=pltpu.CompilerParams(vmem_limit_bytes=VMEM_BYTES),
    )(halves)


def product_kernel(keys, start, finish, me_ref, *refs):
    gram, parts = refs[0], refs[1 : 1 + len(keys)]
    extra = refs[1 + len(keys) : -5]
    out, gbuf, xbuf, acc, sems = refs[-5:]
    count, size, width = xbuf.shape
    h = size // 2

    def piece(j, part):
        return xbuf.at[j, pl.ds(part * h, h)], sems.at[j, part]

    copies = []
    for j in range(count):
        copies.append(pltpu.make_async_copy(gram.at[j], gbuf.at[j], sems.at[j, 2]))
        for part in range(2):
            if keys[0] is None:
                first = pl.multiple_of((me_ref[0] ^ j) * size + part * h, 16)
                source = parts[0].at[pl.ds(first, h), pl.ds(start, width)]
            else:
                key = (j, part * h) if (j, part * h) in keys else (j, 0)
                first = part * h - key[1]
                source = parts[keys.index(key)].at[pl.ds(first, h), pl.ds(start, width)]
            copies.append(pltpu.make_async_copy(source, *piece(j, part)))
    for copy in copies:
        copy.start()
    acc[...] = jnp.zeros_like(acc)

    @pl.loop(0, count)
    def _(j):
        pltpu.make_async_copy(gbuf.at[j], gbuf.at[j], sems.at[j, 2]).wait()
        for part in range(2):
            there, sem = piece(j, part)
            pltpu.make_async_copy(there, there, sem).wait()
        acc[...] += jnp.dot(gbuf[j], xbuf[j], preferred_element_type=f32)

    if finish:
        tile, first = extra
        out[...] = (
            coef_a * tile[...].astype(f32)
            + coef_b * first[...].astype(f32)
            + coef_c * acc[...]
        ).astype(bf16)
    else:
        out[...] = acc[...].astype(bf16)


def product(gram, me, parts, start, width, extra=()):
    count, size, _ = gram.shape
    keys = sorted(parts)
    flops = 2 * count * size * size * width
    return pl.pallas_call(
        functools.partial(product_kernel, keys, start, bool(extra)),
        out_shape=jax.ShapeDtypeStruct((size, width), bf16),
        in_specs=[pl.BlockSpec(memory_space=pltpu.SMEM)]
        + [pl.BlockSpec(memory_space=pl.ANY)] * (1 + len(keys))
        + [pl.BlockSpec(memory_space=pltpu.VMEM)] * len(extra),
        out_specs=pl.BlockSpec(memory_space=pltpu.VMEM),
        scratch_shapes=[
            pltpu.VMEM((count, size, size), bf16),
            pltpu.VMEM((count, size, width), bf16),
            pltpu.VMEM((size, width), f32),
            pltpu.SemaphoreType.DMA((count, 3)),
        ],
        cost_estimate=pl.CostEstimate(
            flops=flops,
            bytes_accessed=2 * count * size * (size + width),
            transcendentals=0,
        ),
        compiler_params=pltpu.CompilerParams(vmem_limit_bytes=VMEM_BYTES),
    )(me.astype(jnp.int32).reshape(1), gram, *[parts[key] for key in keys], *extra)


def per_device(ortho_in):
    rows, cols = ortho_in.shape
    n_row = lax.axis_size("row")
    n_col = lax.axis_size("col")
    me = lax.axis_index("row")
    block = rows * n_col
    width = cols // n_col
    scale = 1.0 / (math.sqrt(block * n_row) + math.sqrt(cols)) ** 2
    h = block // 2
    bit_x, bit_y = n_row // 4, n_row // 2
    cores = range(1, bit_x)
    chips = (bit_x, bit_y, bit_x | bit_y)

    def exchange(value):
        return lax.all_to_all(value, "col", split_axis=0, concat_axis=0, tiled=True)

    tiles, gathered, siblings, tied = [], [], [], []
    start = 0
    thirds = widths_of(width, 3)
    if width % (9 * 256) == 0:
        thirds = [width // 9 * n for n in (3, 4, 2)]
    for k, w in enumerate(thirds):
        first = [start + c * width for c in range(n_col)]
        part = jnp.concatenate([ortho_in[:, f : f + w] for f in first], axis=0)
        if k == 2:
            part = after(part, gathered[0][(bit_x, 0)], gathered[0][(bit_y, 0)])
        tile = exchange(part)
        tiles.append(tile)
        parts, tie = gather_chips(tile)
        gathered.append(parts)
        tied.extend(tie)
        siblings.append(add_cores({(0, 0): tile}))
        start += w

    def low_of(j):
        return ((me & (1 << (j.bit_length() - 1))) == 0).astype(jnp.int32).reshape(1)

    lefts = [[s[(i, 0)] for s in siblings] for i in range(bit_x)]
    jobs = [(0, 0, None, 0), (0, 0, None, h)] + [(0, j, j - 1, 0) for j in cores]
    near = gram_pieces(lefts, jobs, [low_of(j)[0] for j in cores], scale)
    last = near = lax.psum(near, "col")
    gram = start_gram(near, n_row)
    for j in cores:
        theirs = swap(near[1 + j : 2 + j], j)
        gram = put_block(gram, low_of(j), (near, 1 + j), (theirs, 0), j)
    panels = [
        add_cores({**parts, **sibling}) for parts, sibling in zip(gathered, siblings)
    ]
    for stage in (chips[:2], chips[2:]):
        blocks = list(lefts)
        for j in stage:
            peers = [whole_block(parts, j) for parts in gathered]
            if j != chips[-1]:
                peers[0] = after(peers[0], *tied)
            blocks.append(peers)
        jobs = [(i, bit_x + n, n, 0) for n in range(len(stage)) for i in range(bit_x)]
        pieces = gram_pieces(blocks, jobs, [low_of(j)[0] for j in stage], scale)
        held = list(panels[0].values()) if len(stage) == 1 else []
        last = sums = lax.psum(after(pieces, last, *held), "col")
        if len(stage) == 1:
            sums, gram = lax.optimization_barrier((sums, gram))
        for n, j in enumerate(stage):
            theirs = swap(sums[n * bit_x : (n + 1) * bit_x], j)
            gram = put_block(gram, low_of(j), (sums, n * bit_x), (theirs, 0), j)
            for i in cores:
                mine = swap(sums[n * bit_x + i : n * bit_x + i + 1], i)
                gram = put_block(gram, low_of(j), (mine, 0), (theirs, i), j | i)

    outs = []
    for k, w in enumerate(thirds):
        parts = dict(panels[k])
        if k > 0:
            parts[(0, 0)] = after(parts[(0, 0)], first)
        first = product(gram, me, parts, 0, w)
        first_panel = lax.all_gather(first, "row", axis=0, tiled=True)
        if k > 0:
            first_panel = after(first_panel, result)
        result = product(gram, me, {None: first_panel}, 0, w, (tiles[k], first))
        back = lax.all_to_all(result, "col", split_axis=0, concat_axis=1, tiled=True)
        outs.append(back.reshape(rows, n_col, w))
    return jnp.concatenate(outs, axis=2).reshape(rows, cols)


def solution(mesh):
    in_specs = (P(("row", "col"), None),)
    out_specs = P(("row", "col"), None)
    return jax.shard_map(
        per_device, mesh=mesh, in_specs=in_specs, out_specs=out_specs, check_vma=False
    )
```

```python
import functools
import math

import jax
import jax.numpy as jnp
from jax import lax
from jax.experimental import pallas as pl
from jax.experimental.pallas import tpu as pltpu
from jax.sharding import PartitionSpec as P

coef_a = 3.4445
coef_b = -4.775
coef_c = 2.0315
bf16 = jnp.bfloat16
f32 = jnp.float32
VMEM_BYTES = 48 * 1024 * 1024


def widths_of(width, count):
    unit = 256 if width % 256 == 0 else 128
    base, extra = divmod(width // unit, count)
    return [unit * (base + (i >= count - extra)) for i in range(count)]


def dot_t(a, b):
    return lax.dot_general(a, b, (((1,), (1,)), ((), ())), preferred_element_type=f32)


def after(value, *others):
    return lax.optimization_barrier((value, *others))[0]


def swap(value, bit):
    count = lax.axis_size("row")
    return lax.ppermute(value, "row", [(r, r ^ bit) for r in range(count)])


def gather_chips(own):
    count = lax.axis_size("row")
    bit_x, bit_y = count // 4, count // 2
    h = own.shape[0] // 2
    corner = bit_x | bit_y
    parts = {(0, 0): own}
    parts[(bit_x, 0)] = swap(own, bit_x)
    parts[(bit_y, 0)] = swap(own, bit_y)
    from_x, from_y = lax.optimization_barrier((parts[(bit_x, 0)], parts[(bit_y, 0)]))
    upper, lower = lax.optimization_barrier((from_x[:h], from_y[h:]))
    parts[(corner, 0)] = swap(upper, bit_y)
    parts[(corner, h)] = swap(lower, bit_x)
    return parts, (upper, lower)


def add_cores(parts, hold=None):
    bit_x = lax.axis_size("row") // 4
    parts = dict(parts)
    bit = 1
    while bit < bit_x:
        for j, offset in list(parts):
            if (j | bit, offset) not in parts:
                part = parts[(j, offset)]
                if hold is not None:
                    part = after(part, hold)
                parts[(j | bit, offset)] = swap(part, bit)
        bit *= 2
    return parts


def whole_block(parts, j):
    pieces = [parts[key] for key in sorted(parts) if key[0] == j]
    return pieces[0] if len(pieces) == 1 else jnp.concatenate(pieces, axis=0)


def pieces_kernel(count, jobs, scale, low_ref, *refs):
    out = refs[-1]
    h = out.shape[1]

    def product(n, left, right, first):
        total = None
        for k in range(count):
            rows = refs[left * count + k][first : first + h, :]
            term = dot_t(rows, refs[right * count + k][...])
            total = term if total is None else total + term
        out[n] = (total * scale).astype(bf16)

    for n, (left, right, low, first) in enumerate(jobs):
        if low is None:
            product(n, left, right, first)
            continue

        @pl.when(low_ref[low] == 1)
        def _():
            product(n, left, right, 0)

        @pl.when(low_ref[low] == 0)
        def _():
            product(n, right, left, h)


def gram_pieces(blocks, jobs, lows, scale):
    count = len(blocks[0])
    size = blocks[0][0].shape[0]
    width = sum(part.shape[1] for part in blocks[0])
    return pl.pallas_call(
        functools.partial(pieces_kernel, count, jobs, scale),
        out_shape=jax.ShapeDtypeStruct((len(jobs), size // 2, size), bf16),
        in_specs=[pl.BlockSpec(memory_space=pltpu.SMEM)]
        + [pl.BlockSpec(memory_space=pltpu.VMEM)] * (count * len(blocks)),
        out_specs=pl.BlockSpec(memory_space=pltpu.VMEM),
        cost_estimate=pl.CostEstimate(
            flops=len(jobs) * size * size * width,
            bytes_accessed=2 * size * (len(blocks) * width + len(jobs) * size // 2),
            transcendentals=0,
        ),
        compiler_params=pltpu.CompilerParams(vmem_limit_bytes=VMEM_BYTES),
    )(jnp.stack(lows).astype(jnp.int32), *[part for block in blocks for part in block])


def block_kernel(low_ref, mine, theirs, gram_in, out):
    h = mine.shape[0]

    @pl.when(low_ref[0] == 1)
    def _():
        out[:h, :] = mine[...]
        out[h:, :] = theirs[...]

    @pl.when(low_ref[0] == 0)
    def _():
        out[...] = jnp.concatenate([theirs[...], mine[...]], axis=0).T


def put_block(gram, low, mine, theirs, j):
    (mine, m), (theirs, t) = mine, theirs
    _, h, size = mine.shape
    return pl.pallas_call(
        block_kernel,
        grid=(1,),
        out_shape=jax.ShapeDtypeStruct(gram.shape, bf16),
        in_specs=[
            pl.BlockSpec(memory_space=pltpu.SMEM),
            pl.BlockSpec((None, h, size), lambda i: (m, 0, 0)),
            pl.BlockSpec((None, h, size), lambda i: (t, 0, 0)),
            pl.BlockSpec(memory_space=pl.ANY),
        ],
        out_specs=pl.BlockSpec((None, size, size), lambda i: (j, 0, 0)),
        input_output_aliases={3: 0},
        cost_estimate=pl.CostEstimate(
            flops=0, bytes_accessed=4 * size * size, transcendentals=0
        ),
        compiler_params=pltpu.CompilerParams(vmem_limit_bytes=VMEM_BYTES),
    )(low, mine, theirs, gram)


def own_kernel(halves, out):
    h = halves.shape[1]
    out[:h, :] = halves[0]
    out[h:, :] = halves[1]


def start_gram(halves, count):
    _, h, size = halves.shape
    return pl.pallas_call(
        own_kernel,
        grid=(1,),
        out_shape=jax.ShapeDtypeStruct((count, size, size), bf16),
        in_specs=[pl.BlockSpec((2, h, size), lambda i: (0, 0, 0))],
        out_specs=pl.BlockSpec((None, size, size), lambda i: (0, 0, 0)),
        cost_estimate=pl.CostEstimate(
            flops=0, bytes_accessed=4 * size * size, transcendentals=0
        ),
        compiler_params=pltpu.CompilerParams(vmem_limit_bytes=VMEM_BYTES),
    )(halves)


def product_kernel(keys, start, finish, me_ref, *refs):
    gram, parts = refs[0], refs[1 : 1 + len(keys)]
    extra = refs[1 + len(keys) : -5]
    out, gbuf, xbuf, acc, sems = refs[-5:]
    count, size, width = xbuf.shape
    h = size // 2

    def piece(j, part):
        return xbuf.at[j, pl.ds(part * h, h)], sems.at[j, part]

    copies = []
    for j in range(count):
        copies.append(pltpu.make_async_copy(gram.at[j], gbuf.at[j], sems.at[j, 2]))
        for part in range(2):
            if keys[0] is None:
                first = pl.multiple_of((me_ref[0] ^ j) * size + part * h, 16)
                source = parts[0].at[pl.ds(first, h), pl.ds(start, width)]
            else:
                key = (j, part * h) if (j, part * h) in keys else (j, 0)
                first = part * h - key[1]
                source = parts[keys.index(key)].at[pl.ds(first, h), pl.ds(start, width)]
            copies.append(pltpu.make_async_copy(source, *piece(j, part)))
    for copy in copies:
        copy.start()
    acc[...] = jnp.zeros_like(acc)

    @pl.loop(0, count)
    def _(j):
        pltpu.make_async_copy(gbuf.at[j], gbuf.at[j], sems.at[j, 2]).wait()
        for part in range(2):
            there, sem = piece(j, part)
            pltpu.make_async_copy(there, there, sem).wait()
        acc[...] += jnp.dot(gbuf[j], xbuf[j], preferred_element_type=f32)

    if finish:
        tile, first = extra
        out[...] = (
            coef_a * tile[...].astype(f32)
            + coef_b * first[...].astype(f32)
            + coef_c * acc[...]
        ).astype(bf16)
    else:
        out[...] = acc[...].astype(bf16)


def product(gram, me, parts, start, width, extra=()):
    count, size, _ = gram.shape
    keys = sorted(parts)
    flops = 2 * count * size * size * width
    return pl.pallas_call(
        functools.partial(product_kernel, keys, start, bool(extra)),
        out_shape=jax.ShapeDtypeStruct((size, width), bf16),
        in_specs=[pl.BlockSpec(memory_space=pltpu.SMEM)]
        + [pl.BlockSpec(memory_space=pl.ANY)] * (1 + len(keys))
        + [pl.BlockSpec(memory_space=pltpu.VMEM)] * len(extra),
        out_specs=pl.BlockSpec(memory_space=pltpu.VMEM),
        scratch_shapes=[
            pltpu.VMEM((count, size, size), bf16),
            pltpu.VMEM((count, size, width), bf16),
            pltpu.VMEM((size, width), f32),
            pltpu.SemaphoreType.DMA((count, 3)),
        ],
        cost_estimate=pl.CostEstimate(
            flops=flops,
            bytes_accessed=2 * count * size * (size + width),
            transcendentals=0,
        ),
        compiler_params=pltpu.CompilerParams(vmem_limit_bytes=VMEM_BYTES),
    )(me.astype(jnp.int32).reshape(1), gram, *[parts[key] for key in keys], *extra)


def sum_on_line(piece, arrivals):
    count = lax.axis_size("col")
    me = lax.axis_index("col")
    half = count // 2

    def send(stage, value, pairs):
        done = arrivals.setdefault(stage, [])
        if len(done) > 1:
            value = after(value, done[-2])
        arrived = lax.ppermute(value, "col", pairs)
        done.append(arrived)
        return arrived

    def add(left, right):
        return (left.astype(f32) + right.astype(f32)).astype(bf16)

    for s in range(half - 1):
        pairs = [(s, s + 1), (count - 1 - s, count - 2 - s)]
        piece = add(piece, send(s, piece, pairs))
    piece = add(piece, send(half - 1, piece, [(half - 1, half), (half, half - 1)]))
    for s in range(half - 2, -1, -1):
        pairs = [(s + 1, s), (count - 2 - s, count - 1 - s)]
        arrived = send(2 * half - 2 - s, piece, pairs)
        piece = jnp.where((me == s) | (me == count - 1 - s), arrived, piece)
    return piece


def per_device(ortho_in):
    rows, cols = ortho_in.shape
    n_row = lax.axis_size("row")
    n_col = lax.axis_size("col")
    me = lax.axis_index("row")
    block = rows * n_col
    width = cols // n_col
    scale = 1.0 / (math.sqrt(block * n_row) + math.sqrt(cols)) ** 2
    h = block // 2
    bit_x, bit_y = n_row // 4, n_row // 2
    cores = range(1, bit_x)
    chips = (bit_x, bit_y, bit_x | bit_y)

    def exchange(value):
        return lax.all_to_all(value, "col", split_axis=0, concat_axis=0, tiled=True)

    tiles, gathered, siblings, tied = [], [], [], []
    start = 0
    thirds = widths_of(width, 3)
    if width % (9 * 256) == 0:
        thirds = [width // 9 * n for n in (4, 3, 2)]
    for k, w in enumerate(thirds):
        first = [start + c * width for c in range(n_col)]
        part = jnp.concatenate([ortho_in[:, f : f + w] for f in first], axis=0)
        if k == 2:
            part = after(part, gathered[0][(bit_x, 0)], gathered[0][(bit_y, 0)])
        tile = exchange(part)
        tiles.append(tile)
        parts, tie = gather_chips(tile)
        gathered.append(parts)
        tied.extend(tie)
        siblings.append(add_cores({(0, 0): tile}))
        start += w

    def low_of(j):
        return ((me & (1 << (j.bit_length() - 1))) == 0).astype(jnp.int32).reshape(1)

    lefts = [[s[(i, 0)] for s in siblings] for i in range(bit_x)]
    jobs = [(0, 0, None, 0), (0, 0, None, h)] + [(0, j, j - 1, 0) for j in cores]
    near = gram_pieces(lefts, jobs, [low_of(j)[0] for j in cores], scale)
    last = near = lax.psum(near, "col")
    gram = start_gram(near, n_row)
    for j in cores:
        theirs = swap(near[1 + j : 2 + j], j)
        gram = put_block(gram, low_of(j), (near, 1 + j), (theirs, 0), j)
    panels = [
        add_cores({**parts, **sibling}) for parts, sibling in zip(gathered, siblings)
    ]
    corner = chips[-1]
    corners = [part for parts in gathered for key, part in parts.items() if key[0] == corner]

    def chip_pieces(stage, *held):
        blocks = list(lefts)
        for j in stage:
            peers = [whole_block(parts, j) for parts in gathered]
            blocks.append(peers)
        blocks[-1][0] = after(blocks[-1][0], *held) if held else blocks[-1][0]
        jobs = [(i, bit_x + n, n, 0) for n in range(len(stage)) for i in range(bit_x)]
        return gram_pieces(blocks, jobs, [low_of(j)[0] for j in stage], scale)

    sums = lax.psum(after(chip_pieces(chips[:2], *corners), last), "col")
    arrivals = {}
    far = chip_pieces(chips[2:])
    far = [sum_on_line(far[i : i + 1], arrivals) for i in range(bit_x)]
    far_theirs = [swap(piece, corner) for piece in far]
    for i in cores:
        far[i] = swap(far[i], i)
    held = [part for panel in panels[:1] for part in panel.values()]
    sums = after(sums, *far, *far_theirs, *held)
    for i in range(bit_x):
        gram = put_block(gram, low_of(corner), (far[i], 0), (far_theirs[i], 0), corner | i)
    for n, j in enumerate(chips[:2]):
        theirs = swap(sums[n * bit_x : (n + 1) * bit_x], j)
        gram = put_block(gram, low_of(j), (sums, n * bit_x), (theirs, 0), j)
        for i in cores:
            mine = swap(sums[n * bit_x + i : n * bit_x + i + 1], i)
            gram = put_block(gram, low_of(j), (mine, 0), (theirs, i), j | i)

    outs = []
    for k, w in enumerate(thirds):
        parts = dict(panels[k])
        if k > 0:
            parts[(0, 0)] = after(parts[(0, 0)], first)
        first = product(gram, me, parts, 0, w)
        first_panel = lax.all_gather(first, "row", axis=0, tiled=True)
        if k > 0:
            first_panel = after(first_panel, back)
        result = product(gram, me, {None: first_panel}, 0, w, (tiles[k], first))
        back = lax.all_to_all(result, "col", split_axis=0, concat_axis=1, tiled=True)
        outs.append(back.reshape(rows, n_col, w))
    return jnp.concatenate(outs, axis=2).reshape(rows, cols)


def solution(mesh):
    in_specs = (P(("row", "col"), None),)
    out_specs = P(("row", "col"), None)
    return jax.shard_map(
        per_device, mesh=mesh, in_specs=in_specs, out_specs=out_specs, check_vma=False
    )
```

```python
import functools
import math

import jax
import jax.numpy as jnp
from jax import lax
from jax.experimental import pallas as pl
from jax.experimental.pallas import tpu as pltpu
from jax.sharding import PartitionSpec as P

coef_a = 3.4445
coef_b = -4.775
coef_c = 2.0315
bf16 = jnp.bfloat16
f32 = jnp.float32
VMEM_BYTES = 48 * 1024 * 1024


def widths_of(width, count):
    unit = 256 if width % 256 == 0 else 128
    base, extra = divmod(width // unit, count)
    return [unit * (base + (i >= count - extra)) for i in range(count)]


def dot_t(a, b):
    return lax.dot_general(a, b, (((1,), (1,)), ((), ())), preferred_element_type=f32)


def after(value, *others):
    return lax.optimization_barrier((value, *others))[0]


def swap(value, bit):
    count = lax.axis_size("row")
    return lax.ppermute(value, "row", [(r, r ^ bit) for r in range(count)])


def gather_chips(own):
    count = lax.axis_size("row")
    bit_x, bit_y = count // 4, count // 2
    h = own.shape[0] // 2
    corner = bit_x | bit_y
    parts = {(0, 0): own}
    parts[(bit_x, 0)] = swap(own, bit_x)
    parts[(bit_y, 0)] = swap(own, bit_y)
    from_x, from_y = lax.optimization_barrier((parts[(bit_x, 0)], parts[(bit_y, 0)]))
    upper, lower = lax.optimization_barrier((from_x[:h], from_y[h:]))
    parts[(corner, 0)] = swap(upper, bit_y)
    parts[(corner, h)] = swap(lower, bit_x)
    return parts, (upper, lower)


def add_cores(parts, hold=None):
    bit_x = lax.axis_size("row") // 4
    parts = dict(parts)
    bit = 1
    while bit < bit_x:
        for j, offset in list(parts):
            if (j | bit, offset) not in parts:
                part = parts[(j, offset)]
                if hold is not None:
                    part = after(part, hold)
                parts[(j | bit, offset)] = swap(part, bit)
        bit *= 2
    return parts


def whole_block(parts, j):
    pieces = [parts[key] for key in sorted(parts) if key[0] == j]
    return pieces[0] if len(pieces) == 1 else jnp.concatenate(pieces, axis=0)


def pieces_kernel(count, jobs, scale, low_ref, *refs):
    out = refs[-1]
    h = out.shape[1]

    def product(n, left, right, first):
        total = None
        for k in range(count):
            rows = refs[left * count + k][first : first + h, :]
            term = dot_t(rows, refs[right * count + k][...])
            total = term if total is None else total + term
        out[n] = (total * scale).astype(bf16)

    for n, (left, right, low, first) in enumerate(jobs):
        if low is None:
            product(n, left, right, first)
            continue

        @pl.when(low_ref[low] == 1)
        def _():
            product(n, left, right, 0)

        @pl.when(low_ref[low] == 0)
        def _():
            product(n, right, left, h)


def gram_pieces(blocks, jobs, lows, scale):
    count = len(blocks[0])
    size = blocks[0][0].shape[0]
    width = sum(part.shape[1] for part in blocks[0])
    return pl.pallas_call(
        functools.partial(pieces_kernel, count, jobs, scale),
        out_shape=jax.ShapeDtypeStruct((len(jobs), size // 2, size), bf16),
        in_specs=[pl.BlockSpec(memory_space=pltpu.SMEM)]
        + [pl.BlockSpec(memory_space=pltpu.VMEM)] * (count * len(blocks)),
        out_specs=pl.BlockSpec(memory_space=pltpu.VMEM),
        cost_estimate=pl.CostEstimate(
            flops=len(jobs) * size * size * width,
            bytes_accessed=2 * size * (len(blocks) * width + len(jobs) * size // 2),
            transcendentals=0,
        ),
        compiler_params=pltpu.CompilerParams(vmem_limit_bytes=VMEM_BYTES),
    )(jnp.stack(lows).astype(jnp.int32), *[part for block in blocks for part in block])


def block_kernel(low_ref, mine, theirs, gram_in, out):
    h = mine.shape[0]

    @pl.when(low_ref[0] == 1)
    def _():
        out[:h, :] = mine[...]
        out[h:, :] = theirs[...]

    @pl.when(low_ref[0] == 0)
    def _():
        out[...] = jnp.concatenate([theirs[...], mine[...]], axis=0).T


def put_block(gram, low, mine, theirs, j):
    (mine, m), (theirs, t) = mine, theirs
    _, h, size = mine.shape
    return pl.pallas_call(
        block_kernel,
        grid=(1,),
        out_shape=jax.ShapeDtypeStruct(gram.shape, bf16),
        in_specs=[
            pl.BlockSpec(memory_space=pltpu.SMEM),
            pl.BlockSpec((None, h, size), lambda i: (m, 0, 0)),
            pl.BlockSpec((None, h, size), lambda i: (t, 0, 0)),
            pl.BlockSpec(memory_space=pl.ANY),
        ],
        out_specs=pl.BlockSpec((None, size, size), lambda i: (j, 0, 0)),
        input_output_aliases={3: 0},
        cost_estimate=pl.CostEstimate(
            flops=0, bytes_accessed=4 * size * size, transcendentals=0
        ),
        compiler_params=pltpu.CompilerParams(vmem_limit_bytes=VMEM_BYTES),
    )(low, mine, theirs, gram)


def own_kernel(halves, out):
    h = halves.shape[1]
    out[:h, :] = halves[0]
    out[h:, :] = halves[1]


def start_gram(halves, count):
    _, h, size = halves.shape
    return pl.pallas_call(
        own_kernel,
        grid=(1,),
        out_shape=jax.ShapeDtypeStruct((count, size, size), bf16),
        in_specs=[pl.BlockSpec((2, h, size), lambda i: (0, 0, 0))],
        out_specs=pl.BlockSpec((None, size, size), lambda i: (0, 0, 0)),
        cost_estimate=pl.CostEstimate(
            flops=0, bytes_accessed=4 * size * size, transcendentals=0
        ),
        compiler_params=pltpu.CompilerParams(vmem_limit_bytes=VMEM_BYTES),
    )(halves)


def product_kernel(keys, start, finish, n_deps, me_ref, *refs):
    gram, parts = refs[0], refs[1 : 1 + len(keys)]
    extra = refs[1 + len(keys) : -5 - n_deps]
    out, gbuf, xbuf, acc, sems = refs[-5:]
    count, size, width = xbuf.shape
    h = size // 2

    def piece(j, part):
        return xbuf.at[j, pl.ds(part * h, h)], sems.at[j, part]

    copies = []
    for j in range(count):
        copies.append(pltpu.make_async_copy(gram.at[j], gbuf.at[j], sems.at[j, 2]))
        for part in range(2):
            if keys[0] is None:
                first = pl.multiple_of((me_ref[0] ^ j) * size + part * h, 16)
                source = parts[0].at[pl.ds(first, h), pl.ds(start, width)]
            else:
                key = (j, part * h) if (j, part * h) in keys else (j, 0)
                first = part * h - key[1]
                source = parts[keys.index(key)].at[pl.ds(first, h), pl.ds(start, width)]
            copies.append(pltpu.make_async_copy(source, *piece(j, part)))
    for copy in copies:
        copy.start()
    acc[...] = jnp.zeros_like(acc)

    @pl.loop(0, count)
    def _(j):
        pltpu.make_async_copy(gbuf.at[j], gbuf.at[j], sems.at[j, 2]).wait()
        for part in range(2):
            there, sem = piece(j, part)
            pltpu.make_async_copy(there, there, sem).wait()
        acc[...] += jnp.dot(gbuf[j], xbuf[j], preferred_element_type=f32)

    if finish:
        tile, first = extra
        out[...] = (
            coef_a * tile[...].astype(f32)
            + coef_b * first[...].astype(f32)
            + coef_c * acc[...]
        ).astype(bf16)
    else:
        out[...] = acc[...].astype(bf16)


def product(gram, me, parts, start, width, extra=(), deps=()):
    count, size, _ = gram.shape
    keys = sorted(parts)
    flops = 2 * count * size * size * width
    return pl.pallas_call(
        functools.partial(product_kernel, keys, start, bool(extra), len(deps)),
        out_shape=jax.ShapeDtypeStruct((size, width), bf16),
        in_specs=[pl.BlockSpec(memory_space=pltpu.SMEM)]
        + [pl.BlockSpec(memory_space=pl.ANY)] * (1 + len(keys))
        + [pl.BlockSpec(memory_space=pltpu.VMEM)] * len(extra)
        + [pl.BlockSpec(memory_space=pl.ANY)] * len(deps),
        out_specs=pl.BlockSpec(memory_space=pltpu.VMEM),
        scratch_shapes=[
            pltpu.VMEM((count, size, size), bf16),
            pltpu.VMEM((count, size, width), bf16),
            pltpu.VMEM((size, width), f32),
            pltpu.SemaphoreType.DMA((count, 3)),
        ],
        cost_estimate=pl.CostEstimate(
            flops=flops,
            bytes_accessed=2 * count * size * (size + width),
            transcendentals=0,
        ),
        compiler_params=pltpu.CompilerParams(vmem_limit_bytes=VMEM_BYTES),
    )(me.astype(jnp.int32).reshape(1), gram, *[parts[key] for key in keys], *extra, *deps)


def per_device(ortho_in):
    rows, cols = ortho_in.shape
    n_row = lax.axis_size("row")
    n_col = lax.axis_size("col")
    me = lax.axis_index("row")
    block = rows * n_col
    width = cols // n_col
    scale = 1.0 / (math.sqrt(block * n_row) + math.sqrt(cols)) ** 2
    h = block // 2
    bit_x, bit_y = n_row // 4, n_row // 2
    cores = range(1, bit_x)
    chips = (bit_x, bit_y, bit_x | bit_y)

    def exchange(value):
        return lax.all_to_all(value, "col", split_axis=0, concat_axis=0, tiled=True)

    tiles, gathered, siblings, tied = [], [], [], []
    start = 0
    thirds = widths_of(width, 3)
    if width % (9 * 256) == 0:
        thirds = [width // 9 * n for n in (4, 3, 2)]
    for k, w in enumerate(thirds):
        first = [start + c * width for c in range(n_col)]
        part = jnp.concatenate([ortho_in[:, f : f + w] for f in first], axis=0)
        if k == 2:
            part = after(part, gathered[0][(bit_x, 0)], gathered[0][(bit_y, 0)])
        tile = exchange(part)
        tiles.append(tile)
        parts, tie = gather_chips(tile)
        gathered.append(parts)
        tied.extend(tie)
        siblings.append(add_cores({(0, 0): tile}))
        start += w

    def low_of(j):
        return ((me & (1 << (j.bit_length() - 1))) == 0).astype(jnp.int32).reshape(1)

    lefts = [[s[(i, 0)] for s in siblings] for i in range(bit_x)]
    jobs = [(0, 0, None, 0), (0, 0, None, h)] + [(0, j, j - 1, 0) for j in cores]
    near = gram_pieces(lefts, jobs, [low_of(j)[0] for j in cores], scale)
    last = near = lax.psum(near, "col")
    gram = start_gram(near, n_row)
    for j in cores:
        theirs = swap(near[1 + j : 2 + j], j)
        gram = put_block(gram, low_of(j), (near, 1 + j), (theirs, 0), j)
    panels = [
        add_cores({**parts, **sibling}) for parts, sibling in zip(gathered, siblings)
    ]
    for stage in (chips[:2], chips[2:]):
        blocks = list(lefts)
        for j in stage:
            peers = [whole_block(parts, j) for parts in gathered]
            if j != chips[-1]:
                peers[0] = after(peers[0], *tied)
            blocks.append(peers)
        jobs = [(i, bit_x + n, n, 0) for n in range(len(stage)) for i in range(bit_x)]
        pieces = gram_pieces(blocks, jobs, [low_of(j)[0] for j in stage], scale)
        held = list(panels[0].values()) if len(stage) == 1 else []
        last = sums = lax.psum(after(pieces, last, *held), "col")
        if len(stage) == 1:
            sums, gram = lax.optimization_barrier((sums, gram))
        for n, j in enumerate(stage):
            theirs = swap(sums[n * bit_x : (n + 1) * bit_x], j)
            gram = put_block(gram, low_of(j), (sums, n * bit_x), (theirs, 0), j)
            for i in cores:
                mine = swap(sums[n * bit_x + i : n * bit_x + i + 1], i)
                gram = put_block(gram, low_of(j), (mine, 0), (theirs, i), j | i)

    outs, firsts, backs = [], [], []
    for k, w in enumerate(thirds):
        first = product(gram, me, panels[k], 0, w, (), firsts[-1:])
        firsts.append(first)
        first_panel = lax.all_gather(first, "row", axis=0, tiled=True)
        extra = (tiles[k], first)
        result = product(gram, me, {None: first_panel}, 0, w, extra, backs[-1:])
        back = lax.all_to_all(result, "col", split_axis=0, concat_axis=1, tiled=True)
        backs.append(back)
        outs.append(back.reshape(rows, n_col, w))
    return jnp.concatenate(outs, axis=2).reshape(rows, cols)


def solution(mesh):
    in_specs = (P(("row", "col"), None),)
    out_specs = P(("row", "col"), None)
    return jax.shard_map(
        per_device, mesh=mesh, in_specs=in_specs, out_specs=out_specs, check_vma=False
    )
```

```python
import functools
import math

import jax
import jax.numpy as jnp
from jax import lax
from jax.experimental import pallas as pl
from jax.experimental.pallas import tpu as pltpu
from jax.sharding import PartitionSpec as P

coef_a = 3.4445
coef_b = -4.775
coef_c = 2.0315
bf16 = jnp.bfloat16
f32 = jnp.float32
VMEM_BYTES = 48 * 1024 * 1024


def widths_of(width, count):
    unit = 256 if width % 256 == 0 else 128
    base, extra = divmod(width // unit, count)
    return [unit * (base + (i >= count - extra)) for i in range(count)]


def dot_t(a, b):
    return lax.dot_general(a, b, (((1,), (1,)), ((), ())), preferred_element_type=f32)


def after(value, *others):
    return lax.optimization_barrier((value, *others))[0]


def swap(value, bit):
    count = lax.axis_size("row")
    return lax.ppermute(value, "row", [(r, r ^ bit) for r in range(count)])


def gather_chips(own):
    count = lax.axis_size("row")
    bit_x, bit_y = count // 4, count // 2
    h = own.shape[0] // 2
    corner = bit_x | bit_y
    parts = {(0, 0): own}
    parts[(bit_x, 0)] = swap(own, bit_x)
    parts[(bit_y, 0)] = swap(own, bit_y)
    parts[(corner, 0)] = swap(parts[(bit_x, 0)][:h], bit_y)
    parts[(corner, h)] = swap(parts[(bit_y, 0)][h:], bit_x)
    return parts


def add_cores(parts, hold=None):
    bit_x = lax.axis_size("row") // 4
    parts = dict(parts)
    bit = 1
    while bit < bit_x:
        for j, offset in list(parts):
            if (j | bit, offset) not in parts:
                part = parts[(j, offset)]
                if hold is not None:
                    part = after(part, hold)
                parts[(j | bit, offset)] = swap(part, bit)
        bit *= 2
    return parts


def whole_block(parts, j):
    pieces = [parts[key] for key in sorted(parts) if key[0] == j]
    return pieces[0] if len(pieces) == 1 else jnp.concatenate(pieces, axis=0)


def pieces_kernel(count, jobs, scale, low_ref, *refs):
    out = refs[-1]
    h = out.shape[1]

    def product(n, left, right, first):
        total = None
        for k in range(count):
            rows = refs[left * count + k][first : first + h, :]
            term = dot_t(rows, refs[right * count + k][...])
            total = term if total is None else total + term
        out[n] = (total * scale).astype(bf16)

    for n, (left, right, low, first) in enumerate(jobs):
        if low is None:
            product(n, left, right, first)
            continue

        @pl.when(low_ref[low] == 1)
        def _():
            product(n, left, right, 0)

        @pl.when(low_ref[low] == 0)
        def _():
            product(n, right, left, h)


def gram_pieces(blocks, jobs, lows, scale):
    count = len(blocks[0])
    size = blocks[0][0].shape[0]
    width = sum(part.shape[1] for part in blocks[0])
    return pl.pallas_call(
        functools.partial(pieces_kernel, count, jobs, scale),
        out_shape=jax.ShapeDtypeStruct((len(jobs), size // 2, size), bf16),
        in_specs=[pl.BlockSpec(memory_space=pltpu.SMEM)]
        + [pl.BlockSpec(memory_space=pltpu.VMEM)] * (count * len(blocks)),
        out_specs=pl.BlockSpec(memory_space=pltpu.VMEM),
        cost_estimate=pl.CostEstimate(
            flops=len(jobs) * size * size * width,
            bytes_accessed=2 * size * (len(blocks) * width + len(jobs) * size // 2),
            transcendentals=0,
        ),
        compiler_params=pltpu.CompilerParams(vmem_limit_bytes=VMEM_BYTES),
    )(jnp.stack(lows).astype(jnp.int32), *[part for block in blocks for part in block])


def block_kernel(low_ref, mine, theirs, gram_in, out):
    h = mine.shape[0]

    @pl.when(low_ref[0] == 1)
    def _():
        out[:h, :] = mine[...]
        out[h:, :] = theirs[...]

    @pl.when(low_ref[0] == 0)
    def _():
        out[...] = jnp.concatenate([theirs[...], mine[...]], axis=0).T


def put_block(gram, low, mine, theirs, j):
    (mine, m), (theirs, t) = mine, theirs
    _, h, size = mine.shape
    return pl.pallas_call(
        block_kernel,
        grid=(1,),
        out_shape=jax.ShapeDtypeStruct(gram.shape, bf16),
        in_specs=[
            pl.BlockSpec(memory_space=pltpu.SMEM),
            pl.BlockSpec((None, h, size), lambda i: (m, 0, 0)),
            pl.BlockSpec((None, h, size), lambda i: (t, 0, 0)),
            pl.BlockSpec(memory_space=pl.ANY),
        ],
        out_specs=pl.BlockSpec((None, size, size), lambda i: (j, 0, 0)),
        input_output_aliases={3: 0},
        cost_estimate=pl.CostEstimate(
            flops=0, bytes_accessed=4 * size * size, transcendentals=0
        ),
        compiler_params=pltpu.CompilerParams(vmem_limit_bytes=VMEM_BYTES),
    )(low, mine, theirs, gram)


def own_kernel(halves, out):
    h = halves.shape[1]
    out[:h, :] = halves[0]
    out[h:, :] = halves[1]


def start_gram(halves, count):
    _, h, size = halves.shape
    return pl.pallas_call(
        own_kernel,
        grid=(1,),
        out_shape=jax.ShapeDtypeStruct((count, size, size), bf16),
        in_specs=[pl.BlockSpec((2, h, size), lambda i: (0, 0, 0))],
        out_specs=pl.BlockSpec((None, size, size), lambda i: (0, 0, 0)),
        cost_estimate=pl.CostEstimate(
            flops=0, bytes_accessed=4 * size * size, transcendentals=0
        ),
        compiler_params=pltpu.CompilerParams(vmem_limit_bytes=VMEM_BYTES),
    )(halves)


def product_kernel(keys, start, finish, n_deps, me_ref, *refs):
    gram, parts = refs[0], refs[1 : 1 + len(keys)]
    extra = refs[1 + len(keys) : -5 - n_deps]
    out, gbuf, xbuf, acc, sems = refs[-5:]
    count, size, width = xbuf.shape
    h = size // 2

    def piece(j, part):
        return xbuf.at[j, pl.ds(part * h, h)], sems.at[j, part]

    copies = []
    for j in range(count):
        copies.append(pltpu.make_async_copy(gram.at[j], gbuf.at[j], sems.at[j, 2]))
        for part in range(2):
            if keys[0] is None:
                first = pl.multiple_of((me_ref[0] ^ j) * size + part * h, 16)
                source = parts[0].at[pl.ds(first, h), pl.ds(start, width)]
            else:
                key = (j, part * h) if (j, part * h) in keys else (j, 0)
                first = part * h - key[1]
                source = parts[keys.index(key)].at[pl.ds(first, h), pl.ds(start, width)]
            copies.append(pltpu.make_async_copy(source, *piece(j, part)))
    for copy in copies:
        copy.start()
    acc[...] = jnp.zeros_like(acc)

    @pl.loop(0, count)
    def _(j):
        pltpu.make_async_copy(gbuf.at[j], gbuf.at[j], sems.at[j, 2]).wait()
        for part in range(2):
            there, sem = piece(j, part)
            pltpu.make_async_copy(there, there, sem).wait()
        acc[...] += jnp.dot(gbuf[j], xbuf[j], preferred_element_type=f32)

    if finish:
        tile, first = extra
        out[...] = (
            coef_a * tile[...].astype(f32)
            + coef_b * first[...].astype(f32)
            + coef_c * acc[...]
        ).astype(bf16)
    else:
        out[...] = acc[...].astype(bf16)


def product(gram, me, parts, start, width, extra=(), deps=()):
    count, size, _ = gram.shape
    keys = sorted(parts)
    flops = 2 * count * size * size * width
    return pl.pallas_call(
        functools.partial(product_kernel, keys, start, bool(extra), len(deps)),
        out_shape=jax.ShapeDtypeStruct((size, width), bf16),
        in_specs=[pl.BlockSpec(memory_space=pltpu.SMEM)]
        + [pl.BlockSpec(memory_space=pl.ANY)] * (1 + len(keys))
        + [pl.BlockSpec(memory_space=pltpu.VMEM)] * len(extra)
        + [pl.BlockSpec(memory_space=pl.ANY)] * len(deps),
        out_specs=pl.BlockSpec(memory_space=pltpu.VMEM),
        scratch_shapes=[
            pltpu.VMEM((count, size, size), bf16),
            pltpu.VMEM((count, size, width), bf16),
            pltpu.VMEM((size, width), f32),
            pltpu.SemaphoreType.DMA((count, 3)),
        ],
        cost_estimate=pl.CostEstimate(
            flops=flops,
            bytes_accessed=2 * count * size * (size + width),
            transcendentals=0,
        ),
        compiler_params=pltpu.CompilerParams(vmem_limit_bytes=VMEM_BYTES),
    )(me.astype(jnp.int32).reshape(1), gram, *[parts[key] for key in keys], *extra, *deps)


def per_device(ortho_in):
    rows, cols = ortho_in.shape
    n_row = lax.axis_size("row")
    n_col = lax.axis_size("col")
    me = lax.axis_index("row")
    block = rows * n_col
    width = cols // n_col
    scale = 1.0 / (math.sqrt(block * n_row) + math.sqrt(cols)) ** 2
    h = block // 2
    bit_x, bit_y = n_row // 4, n_row // 2
    cores = range(1, bit_x)
    chips = (bit_x, bit_y, bit_x | bit_y)

    def exchange(value):
        return lax.all_to_all(value, "col", split_axis=0, concat_axis=0, tiled=True)

    tiles, siblings = [], []
    start = 0
    thirds = widths_of(width, 3)
    if width % (9 * 256) == 0:
        thirds = [width // 9 * n for n in (3, 4, 2)]
    for w in thirds:
        first = [start + c * width for c in range(n_col)]
        part = jnp.concatenate([ortho_in[:, f : f + w] for f in first], axis=0)
        tile = exchange(part)
        tiles.append(tile)
        siblings.append(add_cores({(0, 0): tile}))
        start += w

    def low_of(j):
        return ((me & (1 << (j.bit_length() - 1))) == 0).astype(jnp.int32).reshape(1)

    lefts = [[s[(i, 0)] for s in siblings] for i in range(bit_x)]
    jobs = [(0, 0, None, 0), (0, 0, None, h)] + [(0, j, j - 1, 0) for j in cores]
    near = gram_pieces(lefts, jobs, [low_of(j)[0] for j in cores], scale)
    gathered = [gather_chips(tile) for tile in tiles[:-1]]
    gathered.append(gather_chips(after(tiles[-1], near)))
    last = near = lax.psum(near, "col")
    gram = start_gram(near, n_row)
    for j in cores:
        theirs = swap(near[1 + j : 2 + j], j)
        gram = put_block(gram, low_of(j), (near, 1 + j), (theirs, 0), j)
    panels = [
        add_cores({**parts, **sibling}) for parts, sibling in zip(gathered, siblings)
    ]
    peers = [[whole_block(parts, j) for parts in gathered] for j in chips]
    lows = [low_of(j)[0] for j in chips]

    def summed(stage, *held):
        used = sorted({n for n, _ in stage})
        blocks = lefts + [peers[n] for n in used]
        jobs = [(i, bit_x + used.index(n), used.index(n), 0) for n, i in stage]
        pieces = gram_pieces(blocks, jobs, [lows[n] for n in used], scale)
        return lax.psum(after(pieces, *held), "col")

    def put_stage(gram, stage, sums):
        for at, (n, i) in enumerate(stage):
            mine = sums[at : at + 1]
            theirs = swap(mine, chips[n])
            if i > 0:
                mine = swap(mine, i)
            gram = put_block(gram, low_of(chips[n]), (mine, 0), (theirs, 0), chips[n] | i)
        return gram

    pairs = [(n, i) for n in range(3) for i in range(bit_x)]
    final = [(n, bit_x - 1) for n in range(2)]
    middle = [pair for pair in pairs if pair not in final]
    last = sums = summed(middle, last)
    gram = put_stage(gram, middle, sums)
    sums = summed(final, last, *panels[1].values())
    sums, gram = lax.optimization_barrier((sums, gram))
    gram = put_stage(gram, final, sums)

    outs, firsts, backs = {}, [], []
    for k in (1, 0, 2):
        w = thirds[k]
        first = product(gram, me, panels[k], 0, w, (), firsts[-1:])
        firsts.append(first)
        first_panel = lax.all_gather(first, "row", axis=0, tiled=True)
        extra = (tiles[k], first)
        result = product(gram, me, {None: first_panel}, 0, w, extra, backs[-1:])
        back = lax.all_to_all(result, "col", split_axis=0, concat_axis=1, tiled=True)
        backs.append(back)
        outs[k] = back.reshape(rows, n_col, w)
    return jnp.concatenate([outs[k] for k in range(3)], axis=2).reshape(rows, cols)


def solution(mesh):
    in_specs = (P(("row", "col"), None),)
    out_specs = P(("row", "col"), None)
    return jax.shard_map(
        per_device, mesh=mesh, in_specs=in_specs, out_specs=out_specs, check_vma=False
    )
```

```python
import functools
import math

import jax
import jax.numpy as jnp
from jax import lax
from jax.experimental import pallas as pl
from jax.experimental.pallas import tpu as pltpu
from jax.sharding import PartitionSpec as P

coef_a = 3.4445
coef_b = -4.775
coef_c = 2.0315
bf16 = jnp.bfloat16
f32 = jnp.float32
VMEM_BYTES = 48 * 1024 * 1024


def widths_of(width, count):
    unit = 256 if width % 256 == 0 else 128
    base, extra = divmod(width // unit, count)
    return [unit * (base + (i >= count - extra)) for i in range(count)]


def dot_t(a, b):
    return lax.dot_general(a, b, (((1,), (1,)), ((), ())), preferred_element_type=f32)


def after(value, *others):
    return lax.optimization_barrier((value, *others))[0]


def swap(value, bit):
    count = lax.axis_size("row")
    return lax.ppermute(value, "row", [(r, r ^ bit) for r in range(count)])


def gather_chips(own):
    count = lax.axis_size("row")
    bit_x, bit_y = count // 4, count // 2
    h = own.shape[0] // 2
    corner = bit_x | bit_y
    parts = {(0, 0): own}
    parts[(bit_x, 0)] = swap(own, bit_x)
    parts[(bit_y, 0)] = swap(own, bit_y)
    from_x, from_y = lax.optimization_barrier((parts[(bit_x, 0)], parts[(bit_y, 0)]))
    upper, lower = lax.optimization_barrier((from_x[:h], from_y[h:]))
    parts[(corner, 0)] = swap(upper, bit_y)
    parts[(corner, h)] = swap(lower, bit_x)
    return parts, (upper, lower)


def add_cores(parts, hold=None):
    bit_x = lax.axis_size("row") // 4
    parts = dict(parts)
    bit = 1
    while bit < bit_x:
        for j, offset in list(parts):
            if (j | bit, offset) not in parts:
                part = parts[(j, offset)]
                if hold is not None:
                    part = after(part, hold)
                parts[(j | bit, offset)] = swap(part, bit)
        bit *= 2
    return parts


def whole_block(parts, j):
    pieces = [parts[key] for key in sorted(parts) if key[0] == j]
    return pieces[0] if len(pieces) == 1 else jnp.concatenate(pieces, axis=0)


def pieces_kernel(count, jobs, scale, low_ref, *refs):
    out = refs[-1]
    h = out.shape[1]

    def product(n, left, right, first):
        total = None
        for k in range(count):
            rows = refs[left * count + k][first : first + h, :]
            term = dot_t(rows, refs[right * count + k][...])
            total = term if total is None else total + term
        out[n] = (total * scale).astype(bf16)

    for n, (left, right, low, first) in enumerate(jobs):
        if low is None:
            product(n, left, right, first)
            continue

        @pl.when(low_ref[low] == 1)
        def _():
            product(n, left, right, 0)

        @pl.when(low_ref[low] == 0)
        def _():
            product(n, right, left, h)


def gram_pieces(blocks, jobs, lows, scale):
    count = len(blocks[0])
    size = blocks[0][0].shape[0]
    width = sum(part.shape[1] for part in blocks[0])
    return pl.pallas_call(
        functools.partial(pieces_kernel, count, jobs, scale),
        out_shape=jax.ShapeDtypeStruct((len(jobs), size // 2, size), bf16),
        in_specs=[pl.BlockSpec(memory_space=pltpu.SMEM)]
        + [pl.BlockSpec(memory_space=pltpu.VMEM)] * (count * len(blocks)),
        out_specs=pl.BlockSpec(memory_space=pltpu.VMEM),
        cost_estimate=pl.CostEstimate(
            flops=len(jobs) * size * size * width,
            bytes_accessed=2 * size * (len(blocks) * width + len(jobs) * size // 2),
            transcendentals=0,
        ),
        compiler_params=pltpu.CompilerParams(vmem_limit_bytes=VMEM_BYTES),
    )(jnp.stack(lows).astype(jnp.int32), *[part for block in blocks for part in block])


def block_kernel(low_ref, mine, theirs, gram_in, out):
    h = mine.shape[0]

    @pl.when(low_ref[0] == 1)
    def _():
        out[:h, :] = mine[...]
        out[h:, :] = theirs[...]

    @pl.when(low_ref[0] == 0)
    def _():
        out[...] = jnp.concatenate([theirs[...], mine[...]], axis=0).T


def put_block(gram, low, mine, theirs, j):
    (mine, m), (theirs, t) = mine, theirs
    _, h, size = mine.shape
    return pl.pallas_call(
        block_kernel,
        grid=(1,),
        out_shape=jax.ShapeDtypeStruct(gram.shape, bf16),
        in_specs=[
            pl.BlockSpec(memory_space=pltpu.SMEM),
            pl.BlockSpec((None, h, size), lambda i: (m, 0, 0)),
            pl.BlockSpec((None, h, size), lambda i: (t, 0, 0)),
            pl.BlockSpec(memory_space=pl.ANY),
        ],
        out_specs=pl.BlockSpec((None, size, size), lambda i: (j, 0, 0)),
        input_output_aliases={3: 0},
        cost_estimate=pl.CostEstimate(
            flops=0, bytes_accessed=4 * size * size, transcendentals=0
        ),
        compiler_params=pltpu.CompilerParams(vmem_limit_bytes=VMEM_BYTES),
    )(low, mine, theirs, gram)


def split_of(size):
    top = -(-(size // 2) // 128) * 128
    return top, size - top


def near_kernel(count, scale, low_ref, *refs):
    out = refs[-1]
    size = out.shape[1]
    h = size // 2
    top, bottom = split_of(size)
    half = bottom // 2

    def product(left, right, rows, columns):
        total = None
        for k in range(count):
            a = refs[left * count + k][rows[0] : rows[1], :]
            b = refs[right * count + k][columns[0] : columns[1], :]
            term = dot_t(a, b)
            total = term if total is None else total + term
        return (total * scale).astype(bf16)

    out[:top, :] = product(0, 0, (0, top), (0, size))
    corner = product(0, 0, (top, size), (top, size))
    out[top : top + half, :bottom] = corner[:half]
    out[top : top + half, bottom : 2 * bottom] = corner[half:]
    out[top : top + half, 2 * bottom :] = jnp.zeros((half, size - 2 * bottom), bf16)
    for j in range(1, len(refs) // count):
        start = top + half + (j - 1) * h

        @pl.when(low_ref[j - 1] == 1)
        def _():
            out[start : start + h, :] = product(0, j, (0, h), (0, size))

        @pl.when(low_ref[j - 1] == 0)
        def _():
            out[start : start + h, :] = product(j, 0, (h, size), (0, size))


def near_pieces(blocks, lows, scale):
    count = len(blocks[0])
    size = blocks[0][0].shape[0]
    width = sum(part.shape[1] for part in blocks[0])
    top, bottom = split_of(size)
    rows = top + bottom // 2 + (len(blocks) - 1) * (size // 2)
    return pl.pallas_call(
        functools.partial(near_kernel, count, scale),
        out_shape=jax.ShapeDtypeStruct((rows, size), bf16),
        in_specs=[pl.BlockSpec(memory_space=pltpu.SMEM)]
        + [pl.BlockSpec(memory_space=pltpu.VMEM)] * (count * len(blocks)),
        out_specs=pl.BlockSpec(memory_space=pltpu.VMEM),
        cost_estimate=pl.CostEstimate(
            flops=2 * rows * size * width,
            bytes_accessed=2 * size * (len(blocks) * width + rows),
            transcendentals=0,
        ),
        compiler_params=pltpu.CompilerParams(vmem_limit_bytes=VMEM_BYTES),
    )(jnp.stack(lows).astype(jnp.int32), *[part for block in blocks for part in block])


def own_kernel(near, out):
    size = out.shape[1]
    top, bottom = split_of(size)
    half = bottom // 2
    out[:top, :] = near[:top, :]
    out[top:, :top] = near[:top, top:].T
    out[top : top + half, top:] = near[top : top + half, :bottom]
    out[top + half :, top:] = near[top : top + half, bottom : 2 * bottom]


def start_gram(near, count):
    rows, size = near.shape
    return pl.pallas_call(
        own_kernel,
        grid=(1,),
        out_shape=jax.ShapeDtypeStruct((count, size, size), bf16),
        in_specs=[pl.BlockSpec((rows, size), lambda i: (0, 0))],
        out_specs=pl.BlockSpec((None, size, size), lambda i: (0, 0, 0)),
        cost_estimate=pl.CostEstimate(
            flops=0, bytes_accessed=4 * size * size, transcendentals=0
        ),
        compiler_params=pltpu.CompilerParams(vmem_limit_bytes=VMEM_BYTES),
    )(near)


def product_kernel(keys, start, finish, n_deps, me_ref, *refs):
    gram, parts = refs[0], refs[1 : 1 + len(keys)]
    extra = refs[1 + len(keys) : -5 - n_deps]
    out, gbuf, xbuf, acc, sems = refs[-5:]
    count, size, width = xbuf.shape
    h = size // 2

    def piece(j, part):
        return xbuf.at[j, pl.ds(part * h, h)], sems.at[j, part]

    copies = []
    for j in range(count):
        copies.append(pltpu.make_async_copy(gram.at[j], gbuf.at[j], sems.at[j, 2]))
        for part in range(2):
            if keys[0] is None:
                first = pl.multiple_of((me_ref[0] ^ j) * size + part * h, 16)
                source = parts[0].at[pl.ds(first, h), pl.ds(start, width)]
            else:
                key = (j, part * h) if (j, part * h) in keys else (j, 0)
                first = part * h - key[1]
                source = parts[keys.index(key)].at[pl.ds(first, h), pl.ds(start, width)]
            copies.append(pltpu.make_async_copy(source, *piece(j, part)))
    for copy in copies:
        copy.start()
    acc[...] = jnp.zeros_like(acc)

    @pl.loop(0, count)
    def _(j):
        pltpu.make_async_copy(gbuf.at[j], gbuf.at[j], sems.at[j, 2]).wait()
        for part in range(2):
            there, sem = piece(j, part)
            pltpu.make_async_copy(there, there, sem).wait()
        acc[...] += jnp.dot(gbuf[j], xbuf[j], preferred_element_type=f32)

    if finish:
        tile, first = extra
        out[...] = (
            coef_a * tile[...].astype(f32)
            + coef_b * first[...].astype(f32)
            + coef_c * acc[...]
        ).astype(bf16)
    else:
        out[...] = acc[...].astype(bf16)


def product(gram, me, parts, start, width, extra=(), deps=()):
    count, size, _ = gram.shape
    keys = sorted(parts)
    flops = 2 * count * size * size * width
    return pl.pallas_call(
        functools.partial(product_kernel, keys, start, bool(extra), len(deps)),
        out_shape=jax.ShapeDtypeStruct((size, width), bf16),
        in_specs=[pl.BlockSpec(memory_space=pltpu.SMEM)]
        + [pl.BlockSpec(memory_space=pl.ANY)] * (1 + len(keys))
        + [pl.BlockSpec(memory_space=pltpu.VMEM)] * len(extra)
        + [pl.BlockSpec(memory_space=pl.ANY)] * len(deps),
        out_specs=pl.BlockSpec(memory_space=pltpu.VMEM),
        scratch_shapes=[
            pltpu.VMEM((count, size, size), bf16),
            pltpu.VMEM((count, size, width), bf16),
            pltpu.VMEM((size, width), f32),
            pltpu.SemaphoreType.DMA((count, 3)),
        ],
        cost_estimate=pl.CostEstimate(
            flops=flops,
            bytes_accessed=2 * count * size * (size + width),
            transcendentals=0,
        ),
        compiler_params=pltpu.CompilerParams(vmem_limit_bytes=VMEM_BYTES),
    )(me.astype(jnp.int32).reshape(1), gram, *[parts[key] for key in keys], *extra, *deps)


def per_device(ortho_in):
    rows, cols = ortho_in.shape
    n_row = lax.axis_size("row")
    n_col = lax.axis_size("col")
    me = lax.axis_index("row")
    block = rows * n_col
    width = cols // n_col
    scale = 1.0 / (math.sqrt(block * n_row) + math.sqrt(cols)) ** 2
    h = block // 2
    bit_x, bit_y = n_row // 4, n_row // 2
    cores = range(1, bit_x)
    chips = (bit_x, bit_y, bit_x | bit_y)

    def exchange(value):
        return lax.all_to_all(value, "col", split_axis=0, concat_axis=0, tiled=True)

    tiles, gathered, siblings, tied = [], [], [], []
    start = 0
    thirds = widths_of(width, 3)
    if width % (9 * 256) == 0:
        thirds = [width // 9 * n for n in (3, 4, 2)]
    for k, w in enumerate(thirds):
        first = [start + c * width for c in range(n_col)]
        part = jnp.concatenate([ortho_in[:, f : f + w] for f in first], axis=0)
        if k == 2:
            part = after(part, gathered[0][(bit_x, 0)], gathered[0][(bit_y, 0)])
        tile = exchange(part)
        tiles.append(tile)
        parts, tie = gather_chips(tile)
        gathered.append(parts)
        tied.extend(tie)
        siblings.append(add_cores({(0, 0): tile}))
        start += w

    def low_of(j):
        return ((me & (1 << (j.bit_length() - 1))) == 0).astype(jnp.int32).reshape(1)

    lefts = [[s[(i, 0)] for s in siblings] for i in range(bit_x)]
    near = near_pieces(lefts, [low_of(j)[0] for j in cores], scale)
    last = near = lax.psum(near, "col")
    gram = start_gram(near, n_row)
    for j in cores:
        start = near.shape[0] - (bit_x - j) * h
        mine = near[start : start + h][None]
        gram = put_block(gram, low_of(j), (mine, 0), (swap(mine, j), 0), j)
    panels = [
        add_cores({**parts, **sibling}) for parts, sibling in zip(gathered, siblings)
    ]
    for stage in (chips[:2], chips[2:]):
        blocks = list(lefts)
        for j in stage:
            peers = [whole_block(parts, j) for parts in gathered]
            if j != chips[-1]:
                peers[0] = after(peers[0], *tied)
            blocks.append(peers)
        jobs = [(i, bit_x + n, n, 0) for n in range(len(stage)) for i in range(bit_x)]
        pieces = gram_pieces(blocks, jobs, [low_of(j)[0] for j in stage], scale)
        held = list(panels[1].values()) if len(stage) == 1 else []
        last = sums = lax.psum(after(pieces, last, *held), "col")
        if len(stage) == 1:
            sums, gram = lax.optimization_barrier((sums, gram))
        for n, j in enumerate(stage):
            theirs = swap(sums[n * bit_x : (n + 1) * bit_x], j)
            gram = put_block(gram, low_of(j), (sums, n * bit_x), (theirs, 0), j)
            for i in cores:
                mine = swap(sums[n * bit_x + i : n * bit_x + i + 1], i)
                gram = put_block(gram, low_of(j), (mine, 0), (theirs, i), j | i)

    outs, firsts, backs = {}, [], []
    for k in (1, 0, 2):
        w = thirds[k]
        first = product(gram, me, panels[k], 0, w, (), firsts[-1:])
        firsts.append(first)
        first_panel = lax.all_gather(first, "row", axis=0, tiled=True)
        extra = (tiles[k], first)
        result = product(gram, me, {None: first_panel}, 0, w, extra, backs[-1:])
        back = lax.all_to_all(result, "col", split_axis=0, concat_axis=1, tiled=True)
        backs.append(back)
        outs[k] = back.reshape(rows, n_col, w)
    return jnp.concatenate([outs[k] for k in range(3)], axis=2).reshape(rows, cols)


def solution(mesh):
    in_specs = (P(("row", "col"), None),)
    out_specs = P(("row", "col"), None)
    return jax.shard_map(
        per_device, mesh=mesh, in_specs=in_specs, out_specs=out_specs, check_vma=False
    )
```

```python
import functools
import math

import jax
import jax.numpy as jnp
from jax import lax
from jax.experimental import pallas as pl
from jax.experimental.pallas import tpu as pltpu
from jax.sharding import PartitionSpec as P

coef_a = 3.4445
coef_b = -4.775
coef_c = 2.0315
bf16 = jnp.bfloat16
f32 = jnp.float32
VMEM_BYTES = 48 * 1024 * 1024


def widths_of(width, count):
    unit = 256 if width % 256 == 0 else 128
    base, extra = divmod(width // unit, count)
    return [unit * (base + (i >= count - extra)) for i in range(count)]


def dot_t(a, b):
    return lax.dot_general(a, b, (((1,), (1,)), ((), ())), preferred_element_type=f32)


def after(value, *others):
    return lax.optimization_barrier((value, *others))[0]


def swap(value, bit):
    count = lax.axis_size("row")
    return lax.ppermute(value, "row", [(r, r ^ bit) for r in range(count)])


def gather_chips(own):
    count = lax.axis_size("row")
    bit_x, bit_y = count // 4, count // 2
    h = own.shape[0] // 2
    corner = bit_x | bit_y
    parts = {(0, 0): own}
    parts[(bit_x, 0)] = swap(own, bit_x)
    parts[(bit_y, 0)] = swap(own, bit_y)
    from_x, from_y = lax.optimization_barrier((parts[(bit_x, 0)], parts[(bit_y, 0)]))
    upper, lower = lax.optimization_barrier((from_x[:h], from_y[h:]))
    parts[(corner, 0)] = swap(upper, bit_y)
    parts[(corner, h)] = swap(lower, bit_x)
    return parts, (upper, lower)


def add_cores(parts, hold=None):
    bit_x = lax.axis_size("row") // 4
    parts = dict(parts)
    bit = 1
    while bit < bit_x:
        for j, offset in list(parts):
            if (j | bit, offset) not in parts:
                part = parts[(j, offset)]
                if hold is not None:
                    part = after(part, hold)
                parts[(j | bit, offset)] = swap(part, bit)
        bit *= 2
    return parts


def whole_block(parts, j):
    pieces = [parts[key] for key in sorted(parts) if key[0] == j]
    return pieces[0] if len(pieces) == 1 else jnp.concatenate(pieces, axis=0)


def pieces_kernel(count, jobs, scale, low_ref, *refs):
    out = refs[-1]
    h = out.shape[1]

    def product(n, left, right, first):
        total = None
        for k in range(count):
            rows = refs[left * count + k][first : first + h, :]
            term = dot_t(rows, refs[right * count + k][...])
            total = term if total is None else total + term
        out[n] = (total * scale).astype(bf16)

    for n, (left, right, low, first) in enumerate(jobs):
        if low is None:
            product(n, left, right, first)
            continue

        @pl.when(low_ref[low] == 1)
        def _():
            product(n, left, right, 0)

        @pl.when(low_ref[low] == 0)
        def _():
            product(n, right, left, h)


def gram_pieces(blocks, jobs, lows, scale):
    count = len(blocks[0])
    size = blocks[0][0].shape[0]
    width = sum(part.shape[1] for part in blocks[0])
    return pl.pallas_call(
        functools.partial(pieces_kernel, count, jobs, scale),
        out_shape=jax.ShapeDtypeStruct((len(jobs), size // 2, size), bf16),
        in_specs=[pl.BlockSpec(memory_space=pltpu.SMEM)]
        + [pl.BlockSpec(memory_space=pltpu.VMEM)] * (count * len(blocks)),
        out_specs=pl.BlockSpec(memory_space=pltpu.VMEM),
        cost_estimate=pl.CostEstimate(
            flops=len(jobs) * size * size * width,
            bytes_accessed=2 * size * (len(blocks) * width + len(jobs) * size // 2),
            transcendentals=0,
        ),
        compiler_params=pltpu.CompilerParams(vmem_limit_bytes=VMEM_BYTES),
    )(jnp.stack(lows).astype(jnp.int32), *[part for block in blocks for part in block])


def block_kernel(low_ref, mine, theirs, gram_in, out):
    h = mine.shape[0]

    @pl.when(low_ref[0] == 1)
    def _():
        out[:h, :] = mine[...]
        out[h:, :] = theirs[...]

    @pl.when(low_ref[0] == 0)
    def _():
        out[...] = jnp.concatenate([theirs[...], mine[...]], axis=0).T


def put_block(gram, low, mine, theirs, j):
    (mine, m), (theirs, t) = mine, theirs
    _, h, size = mine.shape
    return pl.pallas_call(
        block_kernel,
        grid=(1,),
        out_shape=jax.ShapeDtypeStruct(gram.shape, bf16),
        in_specs=[
            pl.BlockSpec(memory_space=pltpu.SMEM),
            pl.BlockSpec((None, h, size), lambda i: (m, 0, 0)),
            pl.BlockSpec((None, h, size), lambda i: (t, 0, 0)),
            pl.BlockSpec(memory_space=pl.ANY),
        ],
        out_specs=pl.BlockSpec((None, size, size), lambda i: (j, 0, 0)),
        input_output_aliases={3: 0},
        cost_estimate=pl.CostEstimate(
            flops=0, bytes_accessed=4 * size * size, transcendentals=0
        ),
        compiler_params=pltpu.CompilerParams(vmem_limit_bytes=VMEM_BYTES),
    )(low, mine, theirs, gram)


def split_of(size):
    top = -(-(size // 2) // 128) * 128
    return top, size - top


def near_kernel(count, scale, low_ref, *refs):
    out = refs[-1]
    size = out.shape[1]
    h = size // 2
    top, bottom = split_of(size)
    half = bottom // 2

    def product(left, right, rows, columns):
        total = None
        for k in range(count):
            a = refs[left * count + k][rows[0] : rows[1], :]
            b = refs[right * count + k][columns[0] : columns[1], :]
            term = dot_t(a, b)
            total = term if total is None else total + term
        return (total * scale).astype(bf16)

    out[:top, :] = product(0, 0, (0, top), (0, size))
    corner = product(0, 0, (top, size), (top, size))
    out[top : top + half, :bottom] = corner[:half]
    out[top : top + half, bottom : 2 * bottom] = corner[half:]
    out[top : top + half, 2 * bottom :] = jnp.zeros((half, size - 2 * bottom), bf16)
    for j in range(1, len(refs) // count):
        start = top + half + (j - 1) * h

        @pl.when(low_ref[j - 1] == 1)
        def _():
            out[start : start + h, :] = product(0, j, (0, h), (0, size))

        @pl.when(low_ref[j - 1] == 0)
        def _():
            out[start : start + h, :] = product(j, 0, (h, size), (0, size))


def near_pieces(blocks, lows, scale):
    count = len(blocks[0])
    size = blocks[0][0].shape[0]
    width = sum(part.shape[1] for part in blocks[0])
    top, bottom = split_of(size)
    rows = top + bottom // 2 + (len(blocks) - 1) * (size // 2)
    return pl.pallas_call(
        functools.partial(near_kernel, count, scale),
        out_shape=jax.ShapeDtypeStruct((rows, size), bf16),
        in_specs=[pl.BlockSpec(memory_space=pltpu.SMEM)]
        + [pl.BlockSpec(memory_space=pltpu.VMEM)] * (count * len(blocks)),
        out_specs=pl.BlockSpec(memory_space=pltpu.VMEM),
        cost_estimate=pl.CostEstimate(
            flops=2 * rows * size * width,
            bytes_accessed=2 * size * (len(blocks) * width + rows),
            transcendentals=0,
        ),
        compiler_params=pltpu.CompilerParams(vmem_limit_bytes=VMEM_BYTES),
    )(jnp.stack(lows).astype(jnp.int32), *[part for block in blocks for part in block])


def own_kernel(near, out):
    size = out.shape[1]
    top, bottom = split_of(size)
    half = bottom // 2
    out[:top, :] = near[:top, :]
    out[top:, :top] = near[:top, top:].T
    out[top : top + half, top:] = near[top : top + half, :bottom]
    out[top + half :, top:] = near[top : top + half, bottom : 2 * bottom]


def start_gram(near, count):
    rows, size = near.shape
    return pl.pallas_call(
        own_kernel,
        grid=(1,),
        out_shape=jax.ShapeDtypeStruct((count, size, size), bf16),
        in_specs=[pl.BlockSpec((rows, size), lambda i: (0, 0))],
        out_specs=pl.BlockSpec((None, size, size), lambda i: (0, 0, 0)),
        cost_estimate=pl.CostEstimate(
            flops=0, bytes_accessed=4 * size * size, transcendentals=0
        ),
        compiler_params=pltpu.CompilerParams(vmem_limit_bytes=VMEM_BYTES),
    )(near)


def product_kernel(keys, start, finish, n_deps, me_ref, *refs):
    gram, parts = refs[0], refs[1 : 1 + len(keys)]
    extra = refs[1 + len(keys) : -5 - n_deps]
    out, gbuf, xbuf, acc, sems = refs[-5:]
    count, size, width = xbuf.shape
    h = size // 2

    def piece(j, part):
        return xbuf.at[j, pl.ds(part * h, h)], sems.at[j, part]

    copies = []
    for j in range(count):
        copies.append(pltpu.make_async_copy(gram.at[j], gbuf.at[j], sems.at[j, 2]))
        for part in range(2):
            if keys[0] is None:
                first = pl.multiple_of((me_ref[0] ^ j) * size + part * h, 16)
                source = parts[0].at[pl.ds(first, h), pl.ds(start, width)]
            else:
                key = (j, part * h) if (j, part * h) in keys else (j, 0)
                first = part * h - key[1]
                source = parts[keys.index(key)].at[pl.ds(first, h), pl.ds(start, width)]
            copies.append(pltpu.make_async_copy(source, *piece(j, part)))
    for copy in copies:
        copy.start()
    acc[...] = jnp.zeros_like(acc)

    @pl.loop(0, count)
    def _(j):
        pltpu.make_async_copy(gbuf.at[j], gbuf.at[j], sems.at[j, 2]).wait()
        for part in range(2):
            there, sem = piece(j, part)
            pltpu.make_async_copy(there, there, sem).wait()
        acc[...] += jnp.dot(gbuf[j], xbuf[j], preferred_element_type=f32)

    if finish:
        tile, first = extra
        out[...] = (
            coef_a * tile[...].astype(f32)
            + coef_b * first[...].astype(f32)
            + coef_c * acc[...]
        ).astype(bf16)
    else:
        out[...] = acc[...].astype(bf16)


def product(gram, me, parts, start, width, extra=(), deps=()):
    count, size, _ = gram.shape
    keys = sorted(parts)
    flops = 2 * count * size * size * width
    return pl.pallas_call(
        functools.partial(product_kernel, keys, start, bool(extra), len(deps)),
        out_shape=jax.ShapeDtypeStruct((size, width), bf16),
        in_specs=[pl.BlockSpec(memory_space=pltpu.SMEM)]
        + [pl.BlockSpec(memory_space=pl.ANY)] * (1 + len(keys))
        + [pl.BlockSpec(memory_space=pltpu.VMEM)] * len(extra)
        + [pl.BlockSpec(memory_space=pl.ANY)] * len(deps),
        out_specs=pl.BlockSpec(memory_space=pltpu.VMEM),
        scratch_shapes=[
            pltpu.VMEM((count, size, size), bf16),
            pltpu.VMEM((count, size, width), bf16),
            pltpu.VMEM((size, width), f32),
            pltpu.SemaphoreType.DMA((count, 3)),
        ],
        cost_estimate=pl.CostEstimate(
            flops=flops,
            bytes_accessed=2 * count * size * (size + width),
            transcendentals=0,
        ),
        compiler_params=pltpu.CompilerParams(vmem_limit_bytes=VMEM_BYTES),
    )(me.astype(jnp.int32).reshape(1), gram, *[parts[key] for key in keys], *extra, *deps)


def sum_on_line(piece, arrivals):
    count = lax.axis_size("col")
    me = lax.axis_index("col")
    half = count // 2

    def send(stage, value, pairs):
        done = arrivals.setdefault(stage, [])
        if len(done) > 1:
            value = after(value, done[-2])
        arrived = lax.ppermute(value, "col", pairs)
        done.append(arrived)
        return arrived

    def add(left, right):
        return (left.astype(f32) + right.astype(f32)).astype(bf16)

    for s in range(half - 1):
        pairs = [(s, s + 1), (count - 1 - s, count - 2 - s)]
        piece = add(piece, send(s, piece, pairs))
    piece = add(piece, send(half - 1, piece, [(half - 1, half), (half, half - 1)]))
    for s in range(half - 2, -1, -1):
        pairs = [(s + 1, s), (count - 2 - s, count - 1 - s)]
        arrived = send(2 * half - 2 - s, piece, pairs)
        piece = jnp.where((me == s) | (me == count - 1 - s), arrived, piece)
    return piece


def per_device(ortho_in):
    rows, cols = ortho_in.shape
    n_row = lax.axis_size("row")
    n_col = lax.axis_size("col")
    me = lax.axis_index("row")
    block = rows * n_col
    width = cols // n_col
    scale = 1.0 / (math.sqrt(block * n_row) + math.sqrt(cols)) ** 2
    h = block // 2
    bit_x, bit_y = n_row // 4, n_row // 2
    cores = range(1, bit_x)
    chips = (bit_x, bit_y, bit_x | bit_y)

    def exchange(value):
        return lax.all_to_all(value, "col", split_axis=0, concat_axis=0, tiled=True)

    tiles, gathered, siblings, tied = [], [], [], []
    start = 0
    thirds = widths_of(width, 3)
    if width % (9 * 256) == 0:
        thirds = [width // 9 * n for n in (3, 4, 2)]
    for k, w in enumerate(thirds):
        first = [start + c * width for c in range(n_col)]
        part = jnp.concatenate([ortho_in[:, f : f + w] for f in first], axis=0)
        if k == 2:
            part = after(part, gathered[0][(bit_x, 0)], gathered[0][(bit_y, 0)])
        tile = exchange(part)
        tiles.append(tile)
        parts, tie = gather_chips(tile)
        gathered.append(parts)
        tied.extend(tie)
        siblings.append(add_cores({(0, 0): tile}))
        start += w

    def low_of(j):
        return ((me & (1 << (j.bit_length() - 1))) == 0).astype(jnp.int32).reshape(1)

    lefts = [[s[(i, 0)] for s in siblings] for i in range(bit_x)]
    near = near_pieces(lefts, [low_of(j)[0] for j in cores], scale)
    last = near = lax.psum(near, "col")
    gram = start_gram(near, n_row)
    for j in cores:
        start = near.shape[0] - (bit_x - j) * h
        mine = near[start : start + h][None]
        gram = put_block(gram, low_of(j), (mine, 0), (swap(mine, j), 0), j)
    panels = [
        add_cores({**parts, **sibling}) for parts, sibling in zip(gathered, siblings)
    ]
    def peers_of(j):
        return [whole_block(parts, j) for parts in gathered]

    blocks = list(lefts)
    for j in chips[:2]:
        peers = peers_of(j)
        peers[0] = after(peers[0], *tied)
        blocks.append(peers)
    jobs = [(i, bit_x + n, n, 0) for n in range(2) for i in range(bit_x)]
    pieces = gram_pieces(blocks, jobs, [low_of(j)[0] for j in chips[:2]], scale)
    last = sums = lax.psum(after(pieces, last), "col")
    for n, j in enumerate(chips[:2]):
        theirs = swap(sums[n * bit_x : (n + 1) * bit_x], j)
        gram = put_block(gram, low_of(j), (sums, n * bit_x), (theirs, 0), j)
        for i in cores:
            mine = swap(sums[n * bit_x + i : n * bit_x + i + 1], i)
            gram = put_block(gram, low_of(j), (mine, 0), (theirs, i), j | i)

    j = chips[-1]
    peers = peers_of(j)
    far = [
        gram_pieces([lefts[i], peers], [(0, 1, 0, 0)], [low_of(j)[0]], scale)
        for i in range(bit_x)
    ]
    arrivals = {}
    lines = {i: sum_on_line(far[i], arrivals) for i in cores}
    sums = lax.psum(after(far[0], last, *panels[1].values()), "col")
    sums, gram = lax.optimization_barrier((sums, gram))
    for i in cores:
        mine, theirs = swap(lines[i], i), swap(lines[i], j)
        gram = put_block(gram, low_of(j), (mine, 0), (theirs, 0), j | i)
    gram = put_block(gram, low_of(j), (sums, 0), (swap(sums, j), 0), j)

    outs, firsts, backs = {}, [], []
    for k in (1, 0, 2):
        w = thirds[k]
        first = product(gram, me, panels[k], 0, w, (), firsts[-1:])
        firsts.append(first)
        first_panel = lax.all_gather(first, "row", axis=0, tiled=True)
        extra = (tiles[k], first)
        result = product(gram, me, {None: first_panel}, 0, w, extra, backs[-1:])
        back = lax.all_to_all(result, "col", split_axis=0, concat_axis=1, tiled=True)
        backs.append(back)
        outs[k] = back.reshape(rows, n_col, w)
    return jnp.concatenate([outs[k] for k in range(3)], axis=2).reshape(rows, cols)


def solution(mesh):
    in_specs = (P(("row", "col"), None),)
    out_specs = P(("row", "col"), None)
    return jax.shard_map(
        per_device, mesh=mesh, in_specs=in_specs, out_specs=out_specs, check_vma=False
    )
```

```python
import functools
import math

import jax
import jax.numpy as jnp
from jax import lax
from jax.experimental import pallas as pl
from jax.experimental.pallas import tpu as pltpu
from jax.sharding import PartitionSpec as P

coef_a = 3.4445
coef_b = -4.775
coef_c = 2.0315
bf16 = jnp.bfloat16
f32 = jnp.float32
VMEM_BYTES = 48 * 1024 * 1024


def widths_of(width, count):
    unit = 256 if width % 256 == 0 else 128
    base, extra = divmod(width // unit, count)
    return [unit * (base + (i >= count - extra)) for i in range(count)]


def dot_t(a, b):
    return lax.dot_general(a, b, (((1,), (1,)), ((), ())), preferred_element_type=f32)


def after(value, *others):
    return lax.optimization_barrier((value, *others))[0]


def swap(value, bit):
    count = lax.axis_size("row")
    return lax.ppermute(value, "row", [(r, r ^ bit) for r in range(count)])


def gather_chips(own):
    count = lax.axis_size("row")
    bit_x, bit_y = count // 4, count // 2
    h = own.shape[0] // 2
    corner = bit_x | bit_y
    parts = {(0, 0): own}
    parts[(bit_x, 0)] = swap(own, bit_x)
    parts[(bit_y, 0)] = swap(own, bit_y)
    from_x, from_y = lax.optimization_barrier((parts[(bit_x, 0)], parts[(bit_y, 0)]))
    upper, lower = lax.optimization_barrier((from_x[:h], from_y[h:]))
    parts[(corner, 0)] = swap(upper, bit_y)
    parts[(corner, h)] = swap(lower, bit_x)
    return parts, (upper, lower)


def add_cores(parts, hold=None):
    bit_x = lax.axis_size("row") // 4
    parts = dict(parts)
    bit = 1
    while bit < bit_x:
        for j, offset in list(parts):
            if (j | bit, offset) not in parts:
                part = parts[(j, offset)]
                if hold is not None:
                    part = after(part, hold)
                parts[(j | bit, offset)] = swap(part, bit)
        bit *= 2
    return parts


def whole_block(parts, j):
    pieces = [parts[key] for key in sorted(parts) if key[0] == j]
    return pieces[0] if len(pieces) == 1 else jnp.concatenate(pieces, axis=0)


def pieces_kernel(count, jobs, scale, low_ref, *refs):
    out = refs[-1]
    h = out.shape[1]

    def product(n, left, right, first):
        total = None
        for k in range(count):
            rows = refs[left * count + k][first : first + h, :]
            term = dot_t(rows, refs[right * count + k][...])
            total = term if total is None else total + term
        out[n] = (total * scale).astype(bf16)

    for n, (left, right, low, first) in enumerate(jobs):
        if low is None:
            product(n, left, right, first)
            continue

        @pl.when(low_ref[low] == 1)
        def _():
            product(n, left, right, 0)

        @pl.when(low_ref[low] == 0)
        def _():
            product(n, right, left, h)


def gram_pieces(blocks, jobs, lows, scale):
    count = len(blocks[0])
    size = blocks[0][0].shape[0]
    width = sum(part.shape[1] for part in blocks[0])
    return pl.pallas_call(
        functools.partial(pieces_kernel, count, jobs, scale),
        out_shape=jax.ShapeDtypeStruct((len(jobs), size // 2, size), bf16),
        in_specs=[pl.BlockSpec(memory_space=pltpu.SMEM)]
        + [pl.BlockSpec(memory_space=pltpu.VMEM)] * (count * len(blocks)),
        out_specs=pl.BlockSpec(memory_space=pltpu.VMEM),
        cost_estimate=pl.CostEstimate(
            flops=len(jobs) * size * size * width,
            bytes_accessed=2 * size * (len(blocks) * width + len(jobs) * size // 2),
            transcendentals=0,
        ),
        compiler_params=pltpu.CompilerParams(vmem_limit_bytes=VMEM_BYTES),
    )(jnp.stack(lows).astype(jnp.int32), *[part for block in blocks for part in block])


def block_kernel(low_ref, mine, theirs, gram_in, out):
    h = mine.shape[0]

    @pl.when(low_ref[0] == 1)
    def _():
        out[:h, :] = mine[...]
        out[h:, :] = theirs[...]

    @pl.when(low_ref[0] == 0)
    def _():
        out[...] = jnp.concatenate([theirs[...], mine[...]], axis=0).T


def put_block(gram, low, mine, theirs, j):
    (mine, m), (theirs, t) = mine, theirs
    _, h, size = mine.shape
    return pl.pallas_call(
        block_kernel,
        grid=(1,),
        out_shape=jax.ShapeDtypeStruct(gram.shape, bf16),
        in_specs=[
            pl.BlockSpec(memory_space=pltpu.SMEM),
            pl.BlockSpec((None, h, size), lambda i: (m, 0, 0)),
            pl.BlockSpec((None, h, size), lambda i: (t, 0, 0)),
            pl.BlockSpec(memory_space=pl.ANY),
        ],
        out_specs=pl.BlockSpec((None, size, size), lambda i: (j, 0, 0)),
        input_output_aliases={3: 0},
        cost_estimate=pl.CostEstimate(
            flops=0, bytes_accessed=4 * size * size, transcendentals=0
        ),
        compiler_params=pltpu.CompilerParams(vmem_limit_bytes=VMEM_BYTES),
    )(low, mine, theirs, gram)


def split_of(size):
    top = -(-(size // 2) // 128) * 128
    return top, size - top


def near_kernel(count, scale, low_ref, *refs):
    out = refs[-1]
    size = out.shape[1]
    h = size // 2
    top, bottom = split_of(size)
    half = bottom // 2

    def product(left, right, rows, columns):
        total = None
        for k in range(count):
            a = refs[left * count + k][rows[0] : rows[1], :]
            b = refs[right * count + k][columns[0] : columns[1], :]
            term = dot_t(a, b)
            total = term if total is None else total + term
        return (total * scale).astype(bf16)

    out[:top, :] = product(0, 0, (0, top), (0, size))
    corner = product(0, 0, (top, size), (top, size))
    out[top : top + half, :bottom] = corner[:half]
    out[top : top + half, bottom : 2 * bottom] = corner[half:]
    out[top : top + half, 2 * bottom :] = jnp.zeros((half, size - 2 * bottom), bf16)
    for j in range(1, len(refs) // count):
        start = top + half + (j - 1) * h

        @pl.when(low_ref[j - 1] == 1)
        def _():
            out[start : start + h, :] = product(0, j, (0, h), (0, size))

        @pl.when(low_ref[j - 1] == 0)
        def _():
            out[start : start + h, :] = product(j, 0, (h, size), (0, size))


def near_pieces(blocks, lows, scale):
    count = len(blocks[0])
    size = blocks[0][0].shape[0]
    width = sum(part.shape[1] for part in blocks[0])
    top, bottom = split_of(size)
    rows = top + bottom // 2 + (len(blocks) - 1) * (size // 2)
    return pl.pallas_call(
        functools.partial(near_kernel, count, scale),
        out_shape=jax.ShapeDtypeStruct((rows, size), bf16),
        in_specs=[pl.BlockSpec(memory_space=pltpu.SMEM)]
        + [pl.BlockSpec(memory_space=pltpu.VMEM)] * (count * len(blocks)),
        out_specs=pl.BlockSpec(memory_space=pltpu.VMEM),
        cost_estimate=pl.CostEstimate(
            flops=2 * rows * size * width,
            bytes_accessed=2 * size * (len(blocks) * width + rows),
            transcendentals=0,
        ),
        compiler_params=pltpu.CompilerParams(vmem_limit_bytes=VMEM_BYTES),
    )(jnp.stack(lows).astype(jnp.int32), *[part for block in blocks for part in block])


def own_kernel(near, out):
    size = out.shape[1]
    top, bottom = split_of(size)
    half = bottom // 2
    out[:top, :] = near[:top, :]
    out[top:, :top] = near[:top, top:].T
    out[top : top + half, top:] = near[top : top + half, :bottom]
    out[top + half :, top:] = near[top : top + half, bottom : 2 * bottom]


def start_gram(near, count):
    rows, size = near.shape
    return pl.pallas_call(
        own_kernel,
        grid=(1,),
        out_shape=jax.ShapeDtypeStruct((count, size, size), bf16),
        in_specs=[pl.BlockSpec((rows, size), lambda i: (0, 0))],
        out_specs=pl.BlockSpec((None, size, size), lambda i: (0, 0, 0)),
        cost_estimate=pl.CostEstimate(
            flops=0, bytes_accessed=4 * size * size, transcendentals=0
        ),
        compiler_params=pltpu.CompilerParams(vmem_limit_bytes=VMEM_BYTES),
    )(near)


def product_kernel(keys, start, finish, n_deps, me_ref, *refs):
    gram, parts = refs[0], refs[1 : 1 + len(keys)]
    extra = refs[1 + len(keys) : -5 - n_deps]
    out, gbuf, xbuf, acc, sems = refs[-5:]
    count, size, width = xbuf.shape
    h = size // 2

    def piece(j, part):
        return xbuf.at[j, pl.ds(part * h, h)], sems.at[j, part]

    copies = []
    for j in range(count):
        copies.append(pltpu.make_async_copy(gram.at[j], gbuf.at[j], sems.at[j, 2]))
        for part in range(2):
            if keys[0] is None:
                first = pl.multiple_of((me_ref[0] ^ j) * size + part * h, 16)
                source = parts[0].at[pl.ds(first, h), pl.ds(start, width)]
            else:
                key = (j, part * h) if (j, part * h) in keys else (j, 0)
                first = part * h - key[1]
                source = parts[keys.index(key)].at[pl.ds(first, h), pl.ds(start, width)]
            copies.append(pltpu.make_async_copy(source, *piece(j, part)))
    for copy in copies:
        copy.start()
    acc[...] = jnp.zeros_like(acc)

    @pl.loop(0, count)
    def _(j):
        pltpu.make_async_copy(gbuf.at[j], gbuf.at[j], sems.at[j, 2]).wait()
        for part in range(2):
            there, sem = piece(j, part)
            pltpu.make_async_copy(there, there, sem).wait()
        acc[...] += jnp.dot(gbuf[j], xbuf[j], preferred_element_type=f32)

    if finish:
        tile, first = extra
        out[...] = (
            coef_a * tile[...].astype(f32)
            + coef_b * first[...].astype(f32)
            + coef_c * acc[...]
        ).astype(bf16)
    else:
        out[...] = acc[...].astype(bf16)


def product(gram, me, parts, start, width, extra=(), deps=()):
    count, size, _ = gram.shape
    keys = sorted(parts)
    flops = 2 * count * size * size * width
    return pl.pallas_call(
        functools.partial(product_kernel, keys, start, bool(extra), len(deps)),
        out_shape=jax.ShapeDtypeStruct((size, width), bf16),
        in_specs=[pl.BlockSpec(memory_space=pltpu.SMEM)]
        + [pl.BlockSpec(memory_space=pl.ANY)] * (1 + len(keys))
        + [pl.BlockSpec(memory_space=pltpu.VMEM)] * len(extra)
        + [pl.BlockSpec(memory_space=pl.ANY)] * len(deps),
        out_specs=pl.BlockSpec(memory_space=pltpu.VMEM),
        scratch_shapes=[
            pltpu.VMEM((count, size, size), bf16),
            pltpu.VMEM((count, size, width), bf16),
            pltpu.VMEM((size, width), f32),
            pltpu.SemaphoreType.DMA((count, 3)),
        ],
        cost_estimate=pl.CostEstimate(
            flops=flops,
            bytes_accessed=2 * count * size * (size + width),
            transcendentals=0,
        ),
        compiler_params=pltpu.CompilerParams(vmem_limit_bytes=VMEM_BYTES),
    )(me.astype(jnp.int32).reshape(1), gram, *[parts[key] for key in keys], *extra, *deps)


def sum_on_line(piece, arrivals):
    count = lax.axis_size("col")
    me = lax.axis_index("col")
    half = count // 2

    def send(stage, value, pairs):
        done = arrivals.setdefault(stage, [])
        if len(done) > 1:
            value = after(value, done[-2])
        arrived = lax.ppermute(value, "col", pairs)
        done.append(arrived)
        return arrived

    def add(left, right):
        return (left.astype(f32) + right.astype(f32)).astype(bf16)

    for s in range(half - 1):
        pairs = [(s, s + 1), (count - 1 - s, count - 2 - s)]
        piece = add(piece, send(s, piece, pairs))
    piece = add(piece, send(half - 1, piece, [(half - 1, half), (half, half - 1)]))
    for s in range(half - 2, -1, -1):
        pairs = [(s + 1, s), (count - 2 - s, count - 1 - s)]
        arrived = send(2 * half - 2 - s, piece, pairs)
        piece = jnp.where((me == s) | (me == count - 1 - s), arrived, piece)
    return piece


def per_device(ortho_in):
    rows, cols = ortho_in.shape
    n_row = lax.axis_size("row")
    n_col = lax.axis_size("col")
    me = lax.axis_index("row")
    block = rows * n_col
    width = cols // n_col
    scale = 1.0 / (math.sqrt(block * n_row) + math.sqrt(cols)) ** 2
    h = block // 2
    bit_x, bit_y = n_row // 4, n_row // 2
    cores = range(1, bit_x)
    chips = (bit_x, bit_y, bit_x | bit_y)

    def exchange(value):
        return lax.all_to_all(value, "col", split_axis=0, concat_axis=0, tiled=True)

    tiles, gathered, siblings, tied = [], [], [], []
    start = 0
    thirds = widths_of(width, 3)
    if width % (9 * 256) == 0:
        thirds = [width // 9 * n for n in (3, 4, 2)]
    for k, w in enumerate(thirds):
        first = [start + c * width for c in range(n_col)]
        part = jnp.concatenate([ortho_in[:, f : f + w] for f in first], axis=0)
        if k == 2:
            part = after(part, gathered[0][(bit_x, 0)], gathered[0][(bit_y, 0)])
        tile = exchange(part)
        tiles.append(tile)
        parts, tie = gather_chips(tile)
        gathered.append(parts)
        tied.extend(tie)
        siblings.append(add_cores({(0, 0): tile}))
        start += w

    def low_of(j):
        return ((me & (1 << (j.bit_length() - 1))) == 0).astype(jnp.int32).reshape(1)

    lefts = [[s[(i, 0)] for s in siblings] for i in range(bit_x)]
    near = near_pieces(lefts, [low_of(j)[0] for j in cores], scale)
    last = near = lax.psum(near, "col")
    gram = start_gram(near, n_row)
    for j in cores:
        start = near.shape[0] - (bit_x - j) * h
        mine = near[start : start + h][None]
        gram = put_block(gram, low_of(j), (mine, 0), (swap(mine, j), 0), j)
    panels = [
        add_cores({**parts, **sibling}) for parts, sibling in zip(gathered, siblings)
    ]
    def peers_of(j):
        return [whole_block(parts, j) for parts in gathered]

    blocks = list(lefts)
    for j in chips[:2]:
        peers = peers_of(j)
        peers[0] = after(peers[0], *tied)
        blocks.append(peers)
    jobs = [(i, bit_x + n, n, 0) for n in range(2) for i in range(bit_x)]
    pieces = gram_pieces(blocks, jobs, [low_of(j)[0] for j in chips[:2]], scale)
    last = sums = lax.psum(after(pieces, last), "col")
    for n, j in enumerate(chips[:2]):
        theirs = swap(sums[n * bit_x : (n + 1) * bit_x], j)
        gram = put_block(gram, low_of(j), (sums, n * bit_x), (theirs, 0), j)
        for i in cores:
            mine = swap(sums[n * bit_x + i : n * bit_x + i + 1], i)
            gram = put_block(gram, low_of(j), (mine, 0), (theirs, i), j | i)

    j = chips[-1]
    peers = peers_of(j)
    jobs = [(i, bit_x, 0, 0) for i in range(bit_x)]
    far = gram_pieces(lefts + [peers], jobs, [low_of(j)[0]], scale)
    far = [far[i : i + 1] for i in range(bit_x)]
    arrivals = {}
    lines = {i: sum_on_line(far[i], arrivals) for i in cores}
    sums = lax.psum(after(far[0], last, *panels[1].values()), "col")
    sums, gram = lax.optimization_barrier((sums, gram))
    for i in cores:
        mine, theirs = swap(lines[i], i), swap(lines[i], j)
        gram = put_block(gram, low_of(j), (mine, 0), (theirs, 0), j | i)
    gram = put_block(gram, low_of(j), (sums, 0), (swap(sums, j), 0), j)

    outs, firsts, backs = {}, [], []
    for k in (1, 0, 2):
        w = thirds[k]
        first = product(gram, me, panels[k], 0, w, (), firsts[-1:])
        firsts.append(first)
        first_panel = lax.all_gather(first, "row", axis=0, tiled=True)
        extra = (tiles[k], first)
        result = product(gram, me, {None: first_panel}, 0, w, extra, backs[-1:])
        back = lax.all_to_all(result, "col", split_axis=0, concat_axis=1, tiled=True)
        backs.append(back)
        outs[k] = back.reshape(rows, n_col, w)
    return jnp.concatenate([outs[k] for k in range(3)], axis=2).reshape(rows, cols)


def solution(mesh):
    in_specs = (P(("row", "col"), None),)
    out_specs = P(("row", "col"), None)
    return jax.shard_map(
        per_device, mesh=mesh, in_specs=in_specs, out_specs=out_specs, check_vma=False
    )
```
